32 devices in a mesh: lat: 2 (over x), lon: 16 (over z, y, core).
Axes of the slice: x: 2, y: 2, z: 4, core: 2. Of those that a mesh axis runs over, the one named last changes fastest.
Arguments:
- field: bfloat16 [128, 512, 128], P('lat', 'lon'), may hold values from -6 to 6
- land_mask: int32 [128, 512], P('lat', 'lon'), may hold values 0 or 1
- zonal_tap_weight: float32 [15, 128], replicated, may hold values from -1.5 to 1.5
- norm_gain: float32 [128], replicated, may hold values from 0.1 to 1.9
- up_weight: bfloat16 [128, 512], replicated, may hold values from -0.5 to 0.5
- down_weight: bfloat16 [512, 128], replicated, may hold values from -0.25 to 0.25
- polar_rows: int32 [64], P('lat'), may hold values from 0 to 63, as said below
- polar_owner: int32 [64], P('lat'), may hold values from 0 to 15, as said below
- polar_taps: float32 [31], replicated, may hold values from -0.8 to 0.8
Outputs:
- mixed_field: bfloat16 [128, 512, 128], P('lat', 'lon')
- polar_field: bfloat16 [128, 512, 128], P(('lat', 'lon'))
The draws below stay inside these ranges and needn't reach their ends.
Inputs may be any that keep to these rules, and one draw needn't show every extreme that they name: `polar_rows`: within each band the 32 entries are distinct rows in increasing order. `polar_owner`: within each band no owner is named by more than 4 entries, and some owner by exactly 4.
All inputs are finite; a program needn't handle non-finite values. No bound on the sum of `land_mask` on one device may be relied on, other than what follows from the above.
Results may differ from the reference program's by a relative error of at most 0.0059.
Values may be sent and summed in bfloat16 or wider, within the bound.
No kernel may reach another device: no remote copies, remote signals or barrier semaphores. Data moves between devices by JAX's collectives and lax.ppermute only.
A program may use at most 64 MiB of HBM per device.

```python
import jax
import jax.numpy as jnp
from jax import lax

C = 128
HID = 512
ZTAPS = 15
DILATION_STEP = 4
FTAPS = 31
LAT_DEV = 64
TILES_LON = 16
NLAT = 128
NLON = 512
PROWS = 32
PROWS_ALL = 64
PMAX = 4
N_LAT = 2
N_LON = 16


def draw_polar_rows(key, part):
    band_count = PROWS_ALL // PROWS

    def one_band(band):
        band_key = jax.random.fold_in(key, band)
        scores = jax.random.permutation(band_key, LAT_DEV)
        row_ids = jnp.arange(LAT_DEV)
        forced = (row_ids == 0) | (row_ids == LAT_DEV - 1)
        scores = jnp.where(forced, -1 - row_ids, scores)
        chosen = jnp.argsort(scores, stable=True)[:PROWS]
        return jnp.sort(chosen)
    picked = jax.vmap(one_band)(jnp.arange(band_count))
    return picked.reshape(-1).astype(jnp.int32)


def draw_polar_owner(key, part):
    band_count = PROWS_ALL // PROWS
    slot_count = TILES_LON * PMAX

    def one_band(band):
        band_key = jax.random.fold_in(jax.random.fold_in(key, 7919), band)
        first_key, second_key, third_key = jax.random.split(band_key, 3)
        drawn_owner = jax.random.randint(first_key, (), 0, TILES_LON)
        full_owner = jnp.where(band == 0, TILES_LON - 1, drawn_owner)
        slot_ids = jnp.arange(slot_count)
        scores = jax.random.permutation(second_key, slot_count)
        scores = jnp.where(slot_ids // PMAX == full_owner, -1 - slot_ids, scores)
        chosen = jnp.argsort(scores, stable=True)[:PROWS]
        owners = chosen // PMAX
        return jax.random.permutation(third_key, owners)
    picked = jax.vmap(one_band)(jnp.arange(band_count))
    return picked.reshape(-1).astype(jnp.int32)


def touch_ends(drawn, stream_key, low, high):
    longest = drawn.shape.index(max(drawn.shape))
    spots = []
    for shift in (0, 1):
        where = [jax.random.randint(jax.random.fold_in(stream_key, axis), (), 0, length) for axis, length in enumerate(drawn.shape)]
        where[longest] = (where[longest] + shift) % drawn.shape[longest]
        spots.append(tuple(where))
    return drawn.at[spots[0]].set(low).at[spots[1]].set(high)


def levels(key, extent, cuts, least, top_value):
    factor_of, own = 1.0, jax.random.fold_in(key, 6)
    for position, parts in cuts:
        draws = jnp.exp(jax.random.uniform(jax.random.fold_in(own, position), (parts,), jnp.float32, least / len(cuts), top_value / len(cuts)))
        factor_of = factor_of * jnp.repeat(draws, extent[position] // parts).reshape([-1 if axis == position else 1 for axis in range(len(extent))])
    return factor_of


def bell_draw(rng, extent, deviation, most, cuts=(), kind=jnp.bfloat16):
    result = deviation * jax.random.normal(rng, extent, jnp.float32)
    if cuts:
        result = result * levels(rng, extent, cuts, -0.22, 0.18)
    return jnp.clip(result, -most, most).astype(kind)


def setup_inputs(seed: int = 0) -> dict:
    key_list = jax.random.split(jax.random.key(seed), 10)
    field = bell_draw(key_list[0], (NLAT, NLON, C), 1.0, 6.0, ((0, 2), (1, 16)))
    land_mask = touch_ends((jax.random.randint(key_list[1], (NLAT, NLON), 0, 4) < 3).astype(jnp.int32), jax.random.fold_in(key_list[1], 1), 0, 1)
    zonal_tap_weight = bell_draw(key_list[2], (ZTAPS, C), ZTAPS ** -0.5, 1.5, (), jnp.float32)
    norm_gain = jnp.clip(1.0 + 0.18 * jax.random.normal(key_list[3], (C,), jnp.float32), 0.1, 1.9)
    up_weight = bell_draw(key_list[4], (C, HID), C ** -0.5, 0.5)
    down_weight = bell_draw(key_list[5], (HID, C), HID ** -0.5, 0.25)
    polar_rows = draw_polar_rows(jax.random.fold_in(key_list[9], 71), 0)
    polar_owner = draw_polar_owner(jax.random.fold_in(key_list[9], 71), 0)
    polar_taps = bell_draw(key_list[8], (FTAPS,), 0.2, 0.8, (), jnp.float32)
    return {"field": field, "land_mask": land_mask, "zonal_tap_weight": zonal_tap_weight, "norm_gain": norm_gain, "up_weight": up_weight, "down_weight": down_weight, "polar_rows": polar_rows, "polar_owner": polar_owner, "polar_taps": polar_taps}


def zonal_mix(block, zonal_tap_weight, norm_gain, up_weight, down_weight):
    source_column = block.astype(jnp.float32)
    tap_sum_output = jnp.zeros(source_column.shape, jnp.float32)
    half_tap_count = zonal_tap_weight.shape[0] // 2
    for zonal_tap_index in range(zonal_tap_weight.shape[0]):
        tap_sum_output = tap_sum_output + zonal_tap_weight[zonal_tap_index] * jnp.roll(source_column, -(zonal_tap_index - half_tap_count) * DILATION_STEP, axis=1)
    average = lax.optimization_barrier(jnp.mean(tap_sum_output, axis=-1, keepdims=True))
    centred = tap_sum_output - average
    variance = lax.optimization_barrier(jnp.mean(centred * centred, axis=-1, keepdims=True))
    normed = (centred * lax.rsqrt(variance + 1e-06) * norm_gain).astype(jnp.bfloat16)
    flat_cells = normed.reshape(-1, normed.shape[-1])
    hidden = jax.nn.gelu(jnp.dot(flat_cells, up_weight, preferred_element_type=jnp.float32)).astype(jnp.bfloat16)
    branch = jnp.dot(hidden, down_weight, preferred_element_type=jnp.float32).astype(jnp.bfloat16)
    return branch.reshape(block.shape)

def reference(field, land_mask, zonal_tap_weight, norm_gain, up_weight, down_weight, polar_rows, polar_owner, polar_taps):
    mask_half = land_mask.astype(jnp.bfloat16)[:, :, None]
    masked = field * mask_half
    block_rows = LAT_DEV // N_LON
    blocks = masked.reshape(NLAT // block_rows, block_rows, NLON, C)
    branch = lax.map(lambda block: zonal_mix(block, zonal_tap_weight, norm_gain, up_weight, down_weight), blocks)
    branch = branch.reshape(NLAT, NLON, C)
    mixed_field = ((masked.astype(jnp.float32) + branch.astype(jnp.float32)) * mask_half.astype(jnp.float32)).astype(jnp.bfloat16)
    entries = jnp.arange(PROWS_ALL).astype(jnp.int32)
    band_index = (entries // PROWS).astype(jnp.int32)
    same_owner = (polar_owner[:, None] == polar_owner[None, :]) & (band_index[:, None] == band_index[None, :]) & (entries[None, :] < entries[:, None])
    slot_rank = lax.optimization_barrier(jnp.sum(same_owner.astype(jnp.int32), axis=1)).astype(jnp.int32)
    destination = ((band_index * N_LON + polar_owner) * PMAX + slot_rank).astype(jnp.int32)
    global_rows = (band_index * LAT_DEV + polar_rows).astype(jnp.int32)
    half_filter = polar_taps.shape[0] // 2

    def filter_row(row_index):
        circle = lax.dynamic_index_in_dim(mixed_field, row_index, 0, keepdims=False).astype(jnp.float32)
        tap_sum_output = jnp.zeros(circle.shape, jnp.float32)
        for zonal_tap_index in range(polar_taps.shape[0]):
            tap_sum_output = tap_sum_output + polar_taps[zonal_tap_index] * jnp.roll(circle, -(zonal_tap_index - half_filter), axis=0)
        return tap_sum_output.astype(jnp.bfloat16)
    filtered = lax.map(filter_row, global_rows)
    polar_field = jnp.zeros((N_LAT * N_LON * PMAX, NLON, C), jnp.bfloat16).at[destination].set(filtered)
    return (mixed_field, polar_field)
```

```python
import functools

import jax
import jax.numpy as jnp
from jax import lax
from jax.experimental import pallas as pl
from jax.experimental.pallas import tpu as pltpu
from jax.sharding import PartitionSpec as P

DILATION_STEP = 4
EXTRA = 16
VMEM_BYTES = 48 * 1024 * 1024
F32 = jnp.float32
BF16 = jnp.bfloat16


def spread_mask(mask_rows, channels):
    n, cols = mask_rows.shape
    eye = (
        lax.broadcasted_iota(jnp.int32, (cols, cols), 0)
        == lax.broadcasted_iota(jnp.int32, (cols, cols), 1)
    ).astype(F32)
    picked = (mask_rows[:, None, :] * eye[None]).astype(BF16).reshape(n * cols, cols)
    return jnp.dot(picked, jnp.ones((cols, channels), BF16), preferred_element_type=F32)


def branch_rows(triples, taps, gain, up, down):
    zonal = []
    n_taps = len(taps)
    for left, own, right in triples:
        cols = own.shape[0]
        start = cols - n_taps // 2 * DILATION_STEP
        line = jnp.concatenate([left, own, right], axis=0).astype(F32)
        aligned = shifted = None
        for k in range(n_taps):
            at = start + k * DILATION_STEP
            if at % 8 == 0:
                term = line[at : at + cols] * taps[k]
                aligned = term if aligned is None else aligned + term
            else:
                term = line[at - 4 : at - 4 + cols + 8] * taps[k]
                shifted = term if shifted is None else shifted + term
        zonal.append(aligned + shifted[4 : 4 + cols])
    zonal = jnp.concatenate(zonal, axis=0)
    mean = jnp.mean(zonal, axis=-1, keepdims=True)
    centred = zonal - mean
    var = jnp.mean(centred * centred, axis=-1, keepdims=True)
    normed = (centred * lax.rsqrt(var + 1e-6) * gain).astype(BF16)
    pre = jnp.dot(normed, up, preferred_element_type=F32)
    inner = pre * (0.7978845608028654 + (0.7978845608028654 * 0.044715) * (pre * pre))
    twice = (pre + pre * jnp.tanh(inner)).astype(BF16)
    return jnp.dot(twice, down, preferred_element_type=F32) * 0.5


def prep_kernel(slots, rows_ref, owner_ref, field_ref, mask_ref, masked_ref, out_ref, count, mask_f, extra):
    lat_rows, cols, channels = field_ref.shape
    tiles = out_ref.shape[0]
    mask_f[...] = jnp.zeros_like(mask_f)
    mask_f[:, :cols] = mask_ref[...].astype(F32)
    extra[...] = jnp.zeros_like(extra)
    out_ref[...] = jnp.zeros_like(out_ref)
    wide = spread_mask(mask_ref[...].astype(F32), channels).astype(BF16)
    masked_ref[...] = field_ref[...] * wide.reshape(lat_rows, cols, channels)
    for tile in range(tiles):
        count[tile] = 0

    def place(e, _):
        owner = owner_ref[e]
        row = rows_ref[e]
        rank = count[owner]
        count[owner] = rank + 1
        out_ref[owner, pl.ds(pl.multiple_of(rank * cols, cols), cols), :] = masked_ref[row]
        extra[pl.ds(owner * EXTRA + rank, 1), :] = mask_f[pl.ds(row, 1), :]
        return 0

    lax.fori_loop(0, owner_ref.shape[0], place, 0, unroll=4)
    out_ref[:, slots * cols :, :] = extra[...].astype(BF16).reshape(tiles, EXTRA, channels)


def prep(field, land_mask, polar_rows, polar_owner, tiles, slots):
    lat_rows, cols, channels = field.shape
    smem = pl.BlockSpec(memory_space=pltpu.SMEM)
    vmem = pl.BlockSpec(memory_space=pltpu.VMEM)
    return pl.pallas_call(
        functools.partial(prep_kernel, slots),
        out_shape=(
            jax.ShapeDtypeStruct(field.shape, BF16),
            jax.ShapeDtypeStruct((tiles, slots * cols + EXTRA, channels), BF16),
        ),
        in_specs=[smem, smem, vmem, vmem],
        out_specs=(vmem, vmem),
        scratch_shapes=[
            pltpu.SMEM((tiles,), jnp.int32),
            pltpu.VMEM((lat_rows, channels), F32),
            pltpu.VMEM((tiles * EXTRA, channels), F32),
        ],
        compiler_params=pltpu.CompilerParams(vmem_limit_bytes=VMEM_BYTES),
        cost_estimate=pl.CostEstimate(flops=10**6, bytes_accessed=2 * 10**6, transcendentals=0),
        name="prep",
    )(polar_rows, polar_owner, field, land_mask)


def tile_kernel(
    chunk, polar_taps_ref, owner_ref, own_ref, cross_ref, swap_ref, mask_ref, taps_ref, gain_ref, up_ref, down_ref,
    mixed_ref, high_ref, low_ref, count_ref, left, right,
):
    lat_rows, cols, channels = own_ref.shape
    me = lax.axis_index("lon")
    odd = lax.rem(me, 2)

    @pl.when(odd == 0)
    def _():
        left[...] = cross_ref[...]
        right[...] = swap_ref[...]

    @pl.when(odd == 1)
    def _():
        left[...] = swap_ref[...]
        right[...] = cross_ref[...]

    def some_rows(step, _):
        at = pl.ds(step * chunk, chunk)
        triples = [(left[step * chunk + r], own_ref[step * chunk + r], right[step * chunk + r]) for r in range(chunk)]
        taps = [taps_ref[k] for k in range(taps_ref.shape[0])]
        taps = [jnp.broadcast_to(t[:1], (1, channels)) for t in taps]
        branch = branch_rows(triples, taps, gain_ref[...], up_ref[...], down_ref[...])
        wide = spread_mask(mask_ref[at, :].astype(F32), channels)
        own = own_ref[at].reshape(chunk * cols, channels).astype(F32)
        mixed = wide * (own + branch.astype(BF16).astype(F32))
        mixed_ref[at] = mixed.astype(BF16).reshape(chunk, cols, channels)
        return 0

    lax.fori_loop(0, lat_rows // chunk, some_rows, 0)

    n, depth = high_ref.shape
    n_taps = polar_taps_ref.shape[0]
    offset = lax.broadcasted_iota(jnp.int32, (n, depth), 1) - lax.broadcasted_iota(jnp.int32, (n, depth), 0)
    first = (depth - n) // 2 - n_taps // 2
    band = jnp.zeros((n, depth), F32)
    for k in range(n_taps):
        band = jnp.where(offset == k + first, polar_taps_ref[k], band)
    high = band.astype(BF16)
    high_ref[...] = high
    low_ref[...] = (band - high.astype(F32)).astype(BF16)
    mine = jnp.int32(0)
    for e in range(owner_ref.shape[0]):
        mine = mine + (owner_ref[e] == me).astype(jnp.int32)
    count_ref[0] = mine


def tile_part(polar_taps, polar_owner, masked, cross, swap, land_mask, weights):
    lat_rows, cols, channels = masked.shape
    smem = pl.BlockSpec(memory_space=pltpu.SMEM)
    vmem = pl.BlockSpec(memory_space=pltpu.VMEM)
    return pl.pallas_call(
        functools.partial(tile_kernel, 8),
        out_shape=(
            jax.ShapeDtypeStruct(masked.shape, BF16),
            jax.ShapeDtypeStruct((128, 160), BF16),
            jax.ShapeDtypeStruct((128, 160), BF16),
            jax.ShapeDtypeStruct((1,), jnp.int32),
        ),
        in_specs=[smem, smem] + [vmem] * 8,
        out_specs=(vmem, vmem, vmem, smem),
        scratch_shapes=[pltpu.VMEM(masked.shape, BF16)] * 2,
        compiler_params=pltpu.CompilerParams(vmem_limit_bytes=VMEM_BYTES),
        cost_estimate=pl.CostEstimate(flops=6 * 10**8, bytes_accessed=3 * 10**6, transcendentals=10**6),
        name="tile",
    )(polar_taps, polar_owner, masked, cross, swap, land_mask, *weights)


def polar_kernel(
    slots, cols, chunk, count_ref, recv_ref, high_ref, low_ref, taps_ref, gain_ref, up_ref, down_ref,
    out_ref, circle,
):
    tiles, _, channels = recv_ref.shape
    n, depth = high_ref.shape
    pad = (depth - n) // 2
    nlon = tiles * cols
    for slot in range(slots):

        @pl.when(slot < count_ref[0])
        def _():
            at = slot * cols

            def some_tiles(step, _):
                def piece(tile):
                    return recv_ref[lax.rem(tile + tiles, tiles), at : at + cols, :]

                base = step * chunk
                pieces = [piece(base + t) for t in range(-1, chunk + 1)]
                triples = [tuple(pieces[t : t + 3]) for t in range(chunk)]
                taps = [jnp.broadcast_to(taps_ref[k][:1], (1, channels)) for k in range(taps_ref.shape[0])]
                branch = branch_rows(triples, taps, gain_ref[...], up_ref[...], down_ref[...])
                extra = recv_ref[pl.ds(base, chunk), slots * cols :, :]
                mask_rows = extra.astype(F32)[:, slot, :cols]
                wide = spread_mask(mask_rows, channels)
                own = jnp.concatenate(pieces[1 : chunk + 1], axis=0).astype(F32)
                mixed = wide * (own + branch.astype(BF16).astype(F32))
                circle[pl.ds(pl.multiple_of(pad + base * cols, 16), chunk * cols), :] = mixed.astype(BF16)
                return 0

            lax.fori_loop(0, tiles // chunk, some_tiles, 0)
            circle[:pad, :] = circle[nlon : nlon + pad, :]
            circle[nlon + pad :, :] = circle[pad : 2 * pad, :]
            for b in range(nlon // n):
                window = circle[b * n : b * n + depth, :]
                out_ref[slot, b * n : (b + 1) * n, :] = (
                    jnp.dot(high_ref[...], window, preferred_element_type=F32)
                    + jnp.dot(low_ref[...], window, preferred_element_type=F32)
                ).astype(BF16)

        @pl.when(slot >= count_ref[0])
        def _():
            out_ref[slot] = jnp.zeros_like(out_ref[slot])


def polar_part(count, recv, high, low, weights, slots, cols):
    tiles, _, channels = recv.shape
    smem = pl.BlockSpec(memory_space=pltpu.SMEM)
    vmem = pl.BlockSpec(memory_space=pltpu.VMEM)
    return pl.pallas_call(
        functools.partial(polar_kernel, slots, cols, 8),
        out_shape=jax.ShapeDtypeStruct((slots, tiles * cols, channels), BF16),
        in_specs=[smem] + [vmem] * 7,
        out_specs=vmem,
        scratch_shapes=[pltpu.VMEM((tiles * cols + 32, channels), BF16)],
        compiler_params=pltpu.CompilerParams(vmem_limit_bytes=VMEM_BYTES),
        cost_estimate=pl.CostEstimate(flops=6 * 10**8, bytes_accessed=2 * 10**6, transcendentals=10**6),
        name="polar",
    )(count, recv, high, low, *weights)


def body(
    field,
    land_mask,
    zonal_tap_weight,
    norm_gain,
    up_weight,
    down_weight,
    polar_rows,
    polar_owner,
    polar_taps,
):
    lat_rows, cols, channels = field.shape
    tiles = lax.axis_size("lon")
    slots = max(2, lat_rows // tiles)
    weights = (
        jnp.broadcast_to(zonal_tap_weight[:, None, :], (zonal_tap_weight.shape[0], 8, channels)),
        norm_gain.reshape(1, channels),
        up_weight,
        down_weight,
    )
    masked, outgoing = prep(field, land_mask, polar_rows, polar_owner, tiles, slots)
    swap_pairs = [(i, i ^ 1) for i in range(tiles)]
    cross_pairs = [(i, (i + 1) % tiles if i % 2 else (i - 1) % tiles) for i in range(tiles)]
    cross = lax.ppermute(masked, "lon", cross_pairs)
    swap = lax.ppermute(masked, "lon", swap_pairs)
    recv = lax.all_to_all(outgoing, "lon", split_axis=0, concat_axis=0, tiled=True)
    mixed, high, low, count = tile_part(polar_taps, polar_owner, masked, cross, swap, land_mask, weights)
    polar = polar_part(count, recv, high, low, weights, slots, cols)
    return (mixed, polar)


def solution(mesh):
    in_specs = (P("lat", "lon", None), P("lat", "lon"), P(), P(), P(), P(), P("lat"), P("lat"), P())
    out_specs = (P("lat", "lon", None), P(("lat", "lon"), None, None))
    return jax.shard_map(body, mesh=mesh, in_specs=in_specs, out_specs=out_specs, check_vma=False)
```

```python
import functools

import jax
import jax.numpy as jnp
from jax import lax
from jax.experimental import pallas as pl
from jax.experimental.pallas import tpu as pltpu
from jax.sharding import PartitionSpec as P

DILATION_STEP = 4
EXTRA = 16
VMEM_BYTES = 48 * 1024 * 1024
F32 = jnp.float32
BF16 = jnp.bfloat16


def spread_mask(mask_rows, channels):
    n, cols = mask_rows.shape
    eye = (
        lax.broadcasted_iota(jnp.int32, (cols, cols), 0)
        == lax.broadcasted_iota(jnp.int32, (cols, cols), 1)
    ).astype(F32)
    picked = (mask_rows[:, None, :] * eye[None]).astype(BF16).reshape(n * cols, cols)
    return jnp.dot(picked, jnp.ones((cols, channels), BF16), preferred_element_type=F32)


def branch_rows(triples, taps, gain, up, down):
    zonal = []
    n_taps = len(taps)
    for left, own, right in triples:
        cols = own.shape[0]
        start = cols - n_taps // 2 * DILATION_STEP
        line = jnp.concatenate([left, own, right], axis=0).astype(F32)
        aligned = shifted = None
        for k in range(n_taps):
            at = start + k * DILATION_STEP
            if at % 8 == 0:
                term = line[at : at + cols] * taps[k]
                aligned = term if aligned is None else aligned + term
            else:
                term = line[at - 4 : at - 4 + cols + 8] * taps[k]
                shifted = term if shifted is None else shifted + term
        zonal.append(aligned + shifted[4 : 4 + cols])
    zonal = jnp.concatenate(zonal, axis=0)
    mean = jnp.mean(zonal, axis=-1, keepdims=True)
    centred = zonal - mean
    var = jnp.mean(centred * centred, axis=-1, keepdims=True)
    normed = (centred * lax.rsqrt(var + 1e-6) * gain).astype(BF16)
    pre = jnp.dot(normed, up, preferred_element_type=F32)
    inner = pre * (0.7978845608028654 + (0.7978845608028654 * 0.044715) * (pre * pre))
    twice = (pre + pre * jnp.tanh(inner)).astype(BF16)
    return jnp.dot(twice, down, preferred_element_type=F32) * 0.5


def prep_kernel(
    slots, rows_ref, owner_ref, field_hbm, mask_ref, masked_ref, out_hbm,
    count, field, mask_f, extra, extra_half, load_sems, row_sems, extra_sem,
):
    lat_rows, cols, channels = field.shape
    tiles = out_hbm.shape[0]
    parts = load_sems.shape[0]
    some = lat_rows // parts
    entries = owner_ref.shape[0]
    loads = [
        pltpu.make_async_copy(field_hbm.at[pl.ds(p * some, some)], field.at[pl.ds(p * some, some)], load_sems.at[p])
        for p in range(parts)
    ]
    for load in loads:
        load.start()
    mask = mask_ref[...].astype(F32).T
    mask_f[...] = jnp.zeros_like(mask_f)
    mask_f[:, :cols] = mask
    extra[...] = jnp.zeros_like(extra)
    for tile in range(tiles):
        count[tile] = 0

    def row_copy(e, row, owner, rank):
        return pltpu.make_async_copy(
            field_hbm.at[row],
            out_hbm.at[owner, pl.ds(pl.multiple_of(rank * cols, cols), cols)],
            row_sems.at[e],
        )

    for e in range(entries):
        owner = owner_ref[e]
        row = rows_ref[e]
        rank = count[owner]
        count[owner] = rank + 1
        row_copy(e, row, owner, rank).start()
        extra[pl.ds(owner * EXTRA + rank, 1), :] = mask_f[pl.ds(row, 1), :]
    extra_half[...] = extra[...].astype(BF16).reshape(tiles, EXTRA, channels)
    extra_copy = pltpu.make_async_copy(extra_half, out_hbm.at[:, pl.ds(slots * cols, EXTRA)], extra_sem)
    extra_copy.start()
    for p, load in enumerate(loads):
        at = slice(p * some, (p + 1) * some)
        wide = spread_mask(mask[at], channels).astype(BF16)
        load.wait()
        masked_ref[at] = field[at] * wide.reshape(some, cols, channels)
    for e in range(entries):
        row_copy(e, 0, 0, 0).wait()
    extra_copy.wait()


def prep(field, land_mask, polar_rows, polar_owner, tiles, slots):
    lat_rows, cols, channels = field.shape
    smem = pl.BlockSpec(memory_space=pltpu.SMEM)
    vmem = pl.BlockSpec(memory_space=pltpu.VMEM)
    hbm = pl.BlockSpec(memory_space=pltpu.HBM)
    return pl.pallas_call(
        functools.partial(prep_kernel, slots),
        out_shape=(
            jax.ShapeDtypeStruct(field.shape, BF16),
            jax.ShapeDtypeStruct((tiles, slots * cols + EXTRA, channels), BF16),
        ),
        in_specs=[smem, smem, hbm, vmem],
        out_specs=(vmem, hbm),
        scratch_shapes=[
            pltpu.SMEM((tiles,), jnp.int32),
            pltpu.VMEM(field.shape, BF16),
            pltpu.VMEM((lat_rows, channels), F32),
            pltpu.VMEM((tiles * EXTRA, channels), F32),
            pltpu.VMEM((tiles, EXTRA, channels), BF16),
            pltpu.SemaphoreType.DMA((4,)),
            pltpu.SemaphoreType.DMA(polar_owner.shape),
            pltpu.SemaphoreType.DMA,
        ],
        compiler_params=pltpu.CompilerParams(vmem_limit_bytes=VMEM_BYTES),
        cost_estimate=pl.CostEstimate(flops=10**6, bytes_accessed=2 * 10**6, transcendentals=0),
        name="prep",
    )(polar_rows, polar_owner, field, land_mask.T)


def tile_kernel(
    chunk, polar_taps_ref, own_ref, cross_ref, swap_ref, mask_ref, taps_ref, gain_ref, up_ref, down_ref,
    mixed_ref, high_ref, low_ref, left, right, mask_f,
):
    lat_rows, cols, channels = own_ref.shape
    me = lax.axis_index("lon")
    odd = lax.rem(me, 2)

    @pl.when(odd == 0)
    def _():
        left[...] = cross_ref[...]
        right[...] = swap_ref[...]

    @pl.when(odd == 1)
    def _():
        left[...] = swap_ref[...]
        right[...] = cross_ref[...]

    mask_f[...] = mask_ref[...].astype(F32).T

    def some_rows(step, _):
        at = pl.ds(step * chunk, chunk)
        triples = [(left[step * chunk + r], own_ref[step * chunk + r], right[step * chunk + r]) for r in range(chunk)]
        taps = [taps_ref[k : k + 1] for k in range(taps_ref.shape[0])]
        branch = branch_rows(triples, taps, gain_ref[...], up_ref[...], down_ref[...])
        wide = spread_mask(mask_f[at, :], channels)
        own = own_ref[at].reshape(chunk * cols, channels).astype(F32)
        mixed = wide * (own + branch.astype(BF16).astype(F32))
        mixed_ref[at] = mixed.astype(BF16).reshape(chunk, cols, channels)
        return 0

    lax.fori_loop(0, lat_rows // chunk, some_rows, 0)

    n, depth = high_ref.shape
    n_taps = polar_taps_ref.shape[0]
    offset = lax.broadcasted_iota(jnp.int32, (n, depth), 1) - lax.broadcasted_iota(jnp.int32, (n, depth), 0)
    first = (depth - n) // 2 - n_taps // 2
    band = jnp.zeros((n, depth), F32)
    for k in range(n_taps):
        band = jnp.where(offset == k + first, polar_taps_ref[k], band)
    high = band.astype(BF16)
    high_ref[...] = high
    low_ref[...] = (band - high.astype(F32)).astype(BF16)


def tile_part(polar_taps, masked, cross, swap, land_mask, weights):
    lat_rows, cols, channels = masked.shape
    smem = pl.BlockSpec(memory_space=pltpu.SMEM)
    vmem = pl.BlockSpec(memory_space=pltpu.VMEM)
    return pl.pallas_call(
        functools.partial(tile_kernel, 32),
        out_shape=(
            jax.ShapeDtypeStruct(masked.shape, BF16),
            jax.ShapeDtypeStruct((128, 160), BF16),
            jax.ShapeDtypeStruct((128, 160), BF16),
        ),
        in_specs=[smem] + [vmem] * 8,
        out_specs=(vmem, vmem, vmem),
        scratch_shapes=[pltpu.VMEM(masked.shape, BF16)] * 2 + [pltpu.VMEM((lat_rows, cols), F32)],
        compiler_params=pltpu.CompilerParams(vmem_limit_bytes=VMEM_BYTES),
        cost_estimate=pl.CostEstimate(flops=5 * 10**9, bytes_accessed=3 * 10**6, transcendentals=10**6),
        name="tile",
    )(polar_taps, masked, cross, swap, land_mask.T, *weights)


def polar_kernel(
    slots, cols, recv_ref, high_ref, low_ref, taps_ref, gain_ref, up_ref, down_ref,
    out_hbm, circle, out, sems,
):
    tiles, _, channels = recv_ref.shape
    n, depth = high_ref.shape
    pad = (depth - n) // 2
    nlon = tiles * cols
    taps = [taps_ref[k : k + 1] for k in range(taps_ref.shape[0])]
    extra = recv_ref[:, slots * cols :, :].astype(F32)
    copies = []
    for slot in range(slots):
        wide = spread_mask(extra[:, slot, :cols], channels)
        recv = jnp.concatenate([recv_ref[t, slot * cols : (slot + 1) * cols, :] for t in range(tiles)], axis=0)
        own = jnp.where(wide > 0.5, recv.astype(F32), 0.0)
        pieces = [own[t * cols : (t + 1) * cols] for t in range(tiles)]
        triples = [(pieces[t - 1], pieces[t], pieces[(t + 1) % tiles]) for t in range(tiles)]
        branch = branch_rows(triples, taps, gain_ref[...], up_ref[...], down_ref[...])
        mixed = (wide * (own + branch.astype(BF16).astype(F32))).astype(BF16)
        circle[slot, pad : nlon + pad, :] = mixed
        circle[slot, :pad, :] = mixed[nlon - pad :]
        circle[slot, nlon + pad :, :] = mixed[:pad]
        for b in range(nlon // n):
            window = circle[slot, b * n : b * n + depth, :]
            out[slot, b * n : (b + 1) * n, :] = (
                jnp.dot(high_ref[...], window, preferred_element_type=F32)
                + jnp.dot(low_ref[...], window, preferred_element_type=F32)
            ).astype(BF16)
        copies.append(pltpu.make_async_copy(out.at[slot], out_hbm.at[slot], sems.at[slot]))
        copies[-1].start()
    for copy in copies:
        copy.wait()


def polar_part(recv, high, low, weights, slots, cols):
    tiles, _, channels = recv.shape
    vmem = pl.BlockSpec(memory_space=pltpu.VMEM)
    shape = (slots, tiles * cols, channels)
    return pl.pallas_call(
        functools.partial(polar_kernel, slots, cols),
        out_shape=jax.ShapeDtypeStruct(shape, BF16),
        in_specs=[vmem] * 7,
        out_specs=pl.BlockSpec(memory_space=pltpu.HBM),
        scratch_shapes=[
            pltpu.VMEM((slots, tiles * cols + 32, channels), BF16),
            pltpu.VMEM(shape, BF16),
            pltpu.SemaphoreType.DMA((slots,)),
        ],
        compiler_params=pltpu.CompilerParams(vmem_limit_bytes=VMEM_BYTES),
        cost_estimate=pl.CostEstimate(flops=6 * 10**8, bytes_accessed=2 * 10**6, transcendentals=10**6),
        name="polar",
    )(recv, high, low, *weights)


def body(
    field,
    land_mask,
    zonal_tap_weight,
    norm_gain,
    up_weight,
    down_weight,
    polar_rows,
    polar_owner,
    polar_taps,
):
    lat_rows, cols, channels = field.shape
    tiles = lax.axis_size("lon")
    slots = max(2, lat_rows // tiles)
    weights = (
        zonal_tap_weight,
        norm_gain.reshape(1, channels),
        up_weight,
        down_weight,
    )
    masked, outgoing = prep(field, land_mask, polar_rows, polar_owner, tiles, slots)
    swap_pairs = [(i, i ^ 1) for i in range(tiles)]
    cross_pairs = [(i, (i + 1) % tiles if i % 2 else (i - 1) % tiles) for i in range(tiles)]
    cross = lax.ppermute(masked, "lon", cross_pairs)
    swap = lax.ppermute(masked, "lon", swap_pairs)
    recv = lax.all_to_all(outgoing, "lon", split_axis=0, concat_axis=0, tiled=True)
    mixed, high, low = tile_part(polar_taps, masked, cross, swap, land_mask, weights)
    polar = polar_part(recv, high, low, weights, slots, cols)
    return (mixed, polar)


def solution(mesh):
    in_specs = (P("lat", "lon", None), P("lat", "lon"), P(), P(), P(), P(), P("lat"), P("lat"), P())
    out_specs = (P("lat", "lon", None), P(("lat", "lon"), None, None))
    return jax.shard_map(body, mesh=mesh, in_specs=in_specs, out_specs=out_specs, check_vma=False)
```

```python
import functools

import jax
import jax.numpy as jnp
from jax import lax
from jax.experimental import pallas as pl
from jax.experimental.pallas import tpu as pltpu
from jax.sharding import PartitionSpec as P

DILATION_STEP = 4
EXTRA = 16
VMEM_BYTES = 48 * 1024 * 1024
F32 = jnp.float32
BF16 = jnp.bfloat16


def spread_mask(mask_rows, channels):
    n, cols = mask_rows.shape
    eye = (
        lax.broadcasted_iota(jnp.int32, (cols, cols), 0)
        == lax.broadcasted_iota(jnp.int32, (cols, cols), 1)
    ).astype(F32)
    picked = (mask_rows[:, None, :] * eye[None]).astype(BF16).reshape(n * cols, cols)
    return jnp.dot(picked, jnp.ones((cols, channels), BF16), preferred_element_type=F32)


def branch_rows(triples, taps, gain, up, down):
    zonal = []
    n_taps = len(taps)
    for left, own, right in triples:
        cols = own.shape[0]
        start = cols - n_taps // 2 * DILATION_STEP
        line = jnp.concatenate([left, own, right], axis=0).astype(F32)
        aligned = shifted = None
        for k in range(n_taps):
            at = start + k * DILATION_STEP
            if at % 8 == 0:
                term = line[at : at + cols] * taps[k]
                aligned = term if aligned is None else aligned + term
            else:
                term = line[at - 4 : at - 4 + cols + 8] * taps[k]
                shifted = term if shifted is None else shifted + term
        zonal.append(aligned + shifted[4 : 4 + cols])
    zonal = jnp.concatenate(zonal, axis=0)
    mean = jnp.mean(zonal, axis=-1, keepdims=True)
    centred = zonal - mean
    var = jnp.mean(centred * centred, axis=-1, keepdims=True)
    normed = (centred * lax.rsqrt(var + 1e-6) * gain).astype(BF16)
    pre = jnp.dot(normed, up, preferred_element_type=F32)
    inner = pre * (0.7978845608028654 + (0.7978845608028654 * 0.044715) * (pre * pre))
    twice = (pre + pre * jnp.tanh(inner)).astype(BF16)
    return jnp.dot(twice, down, preferred_element_type=F32) * 0.5


def prep_kernel(
    slots, rows_ref, owner_ref, field_hbm, mask_ref, masked_ref, out_hbm,
    count, field, mask_f, extra, extra_half, load_sems, row_sems, extra_sem,
):
    lat_rows, cols, channels = field.shape
    tiles = out_hbm.shape[0]
    parts = load_sems.shape[0]
    some = lat_rows // parts
    entries = owner_ref.shape[0]
    loads = [
        pltpu.make_async_copy(field_hbm.at[pl.ds(p * some, some)], field.at[pl.ds(p * some, some)], load_sems.at[p])
        for p in range(parts)
    ]
    for load in loads:
        load.start()
    mask = mask_ref[...].astype(F32).T
    mask_f[...] = jnp.zeros_like(mask_f)
    mask_f[:, :cols] = mask
    extra[...] = jnp.zeros_like(extra)
    for tile in range(tiles):
        count[tile] = 0

    def row_copy(e, row, owner, rank):
        return pltpu.make_async_copy(
            masked_ref.at[row],
            out_hbm.at[owner, pl.ds(pl.multiple_of(rank * cols, cols), cols)],
            row_sems.at[e],
        )

    places = []
    for e in range(entries):
        owner = owner_ref[e]
        row = rows_ref[e]
        rank = count[owner]
        count[owner] = rank + 1
        extra[pl.ds(owner * EXTRA + rank, 1), :] = mask_f[pl.ds(row, 1), :]
        places.append((row, owner, rank))
    extra_half[...] = extra[...].astype(BF16).reshape(tiles, EXTRA, channels)
    extra_copy = pltpu.make_async_copy(extra_half, out_hbm.at[:, pl.ds(slots * cols, EXTRA)], extra_sem)
    extra_copy.start()
    for p, load in enumerate(loads):
        at = slice(p * some, (p + 1) * some)
        wide = spread_mask(mask[at], channels).astype(BF16)
        load.wait()
        masked_ref[at] = field[at] * wide.reshape(some, cols, channels)
    for e, place in enumerate(places):
        row_copy(e, *place).start()
    for e, place in enumerate(places):
        row_copy(e, *place).wait()
    extra_copy.wait()


def prep(field, land_mask, polar_rows, polar_owner, tiles, slots):
    lat_rows, cols, channels = field.shape
    smem = pl.BlockSpec(memory_space=pltpu.SMEM)
    vmem = pl.BlockSpec(memory_space=pltpu.VMEM)
    hbm = pl.BlockSpec(memory_space=pltpu.HBM)
    return pl.pallas_call(
        functools.partial(prep_kernel, slots),
        out_shape=(
            jax.ShapeDtypeStruct(field.shape, BF16),
            jax.ShapeDtypeStruct((tiles, slots * cols + EXTRA, channels), BF16),
        ),
        in_specs=[smem, smem, hbm, vmem],
        out_specs=(vmem, hbm),
        scratch_shapes=[
            pltpu.SMEM((tiles,), jnp.int32),
            pltpu.VMEM(field.shape, BF16),
            pltpu.VMEM((lat_rows, channels), F32),
            pltpu.VMEM((tiles * EXTRA, channels), F32),
            pltpu.VMEM((tiles, EXTRA, channels), BF16),
            pltpu.SemaphoreType.DMA((4,)),
            pltpu.SemaphoreType.DMA(polar_owner.shape),
            pltpu.SemaphoreType.DMA,
        ],
        cost_estimate=pl.CostEstimate(flops=10**6, bytes_accessed=2 * 10**6, transcendentals=0),
        name="prep",
    )(polar_rows, polar_owner, field, land_mask.T)


def tile_kernel(
    chunk, polar_taps_ref, own_ref, cross_ref, swap_ref, mask_ref, taps_ref, gain_ref, up_ref, down_ref,
    mixed_ref, high_ref, low_ref, left, right, mask_f,
):
    lat_rows, cols, channels = own_ref.shape
    me = lax.axis_index("lon")
    odd = lax.rem(me, 2)

    @pl.when(odd == 0)
    def _():
        left[...] = cross_ref[...]
        right[...] = swap_ref[...]

    @pl.when(odd == 1)
    def _():
        left[...] = swap_ref[...]
        right[...] = cross_ref[...]

    mask_f[...] = mask_ref[...].astype(F32).T

    def some_rows(step, _):
        at = pl.ds(step * chunk, chunk)
        triples = [(left[step * chunk + r], own_ref[step * chunk + r], right[step * chunk + r]) for r in range(chunk)]
        taps = [taps_ref[k : k + 1] for k in range(taps_ref.shape[0])]
        branch = branch_rows(triples, taps, gain_ref[...], up_ref[...], down_ref[...])
        wide = spread_mask(mask_f[at, :], channels)
        own = own_ref[at].reshape(chunk * cols, channels).astype(F32)
        mixed = wide * (own + branch.astype(BF16).astype(F32))
        mixed_ref[at] = mixed.astype(BF16).reshape(chunk, cols, channels)
        return 0

    lax.fori_loop(0, lat_rows // chunk, some_rows, 0)

    n, depth = high_ref.shape
    n_taps = polar_taps_ref.shape[0]
    offset = lax.broadcasted_iota(jnp.int32, (n, depth), 1) - lax.broadcasted_iota(jnp.int32, (n, depth), 0)
    first = (depth - n) // 2 - n_taps // 2
    band = jnp.zeros((n, depth), F32)
    for k in range(n_taps):
        band = jnp.where(offset == k + first, polar_taps_ref[k], band)
    high = band.astype(BF16)
    high_ref[...] = high
    low_ref[...] = (band - high.astype(F32)).astype(BF16)


def tile_part(polar_taps, masked, cross, swap, land_mask, weights):
    lat_rows, cols, channels = masked.shape
    smem = pl.BlockSpec(memory_space=pltpu.SMEM)
    vmem = pl.BlockSpec(memory_space=pltpu.VMEM)
    return pl.pallas_call(
        functools.partial(tile_kernel, 32),
        out_shape=(
            jax.ShapeDtypeStruct(masked.shape, BF16),
            jax.ShapeDtypeStruct((128, 160), BF16),
            jax.ShapeDtypeStruct((128, 160), BF16),
        ),
        in_specs=[smem] + [vmem] * 8,
        out_specs=(vmem, vmem, vmem),
        scratch_shapes=[pltpu.VMEM(masked.shape, BF16)] * 2 + [pltpu.VMEM((lat_rows, cols), F32)],
        compiler_params=pltpu.CompilerParams(vmem_limit_bytes=VMEM_BYTES),
        cost_estimate=pl.CostEstimate(flops=5 * 10**10, bytes_accessed=3 * 10**6, transcendentals=10**6),
        name="tile",
    )(polar_taps, masked, cross, swap, land_mask.T, *weights)


def polar_kernel(
    slots, cols, recv_ref, high_ref, low_ref, taps_ref, gain_ref, up_ref, down_ref,
    out_hbm, circle, out, sems,
):
    tiles, _, channels = recv_ref.shape
    n, depth = high_ref.shape
    pad = (depth - n) // 2
    nlon = tiles * cols
    taps = [taps_ref[k : k + 1] for k in range(taps_ref.shape[0])]
    extra = recv_ref[:, slots * cols :, :].astype(F32)
    copies = []
    for slot in range(slots):
        wide = spread_mask(extra[:, slot, :cols], channels)
        recv = jnp.concatenate([recv_ref[t, slot * cols : (slot + 1) * cols, :] for t in range(tiles)], axis=0)
        own = jnp.where(wide > 0.5, recv.astype(F32), 0.0)
        pieces = [own[t * cols : (t + 1) * cols] for t in range(tiles)]
        triples = [(pieces[t - 1], pieces[t], pieces[(t + 1) % tiles]) for t in range(tiles)]
        branch = branch_rows(triples, taps, gain_ref[...], up_ref[...], down_ref[...])
        mixed = (wide * (own + branch.astype(BF16).astype(F32))).astype(BF16)
        circle[slot, pad : nlon + pad, :] = mixed
        circle[slot, :pad, :] = mixed[nlon - pad :]
        circle[slot, nlon + pad :, :] = mixed[:pad]
        for b in range(nlon // n):
            window = circle[slot, b * n : b * n + depth, :]
            out[slot, b * n : (b + 1) * n, :] = (
                jnp.dot(high_ref[...], window, preferred_element_type=F32)
                + jnp.dot(low_ref[...], window, preferred_element_type=F32)
            ).astype(BF16)
        copies.append(pltpu.make_async_copy(out.at[slot], out_hbm.at[slot], sems.at[slot]))
        copies[-1].start()
    for copy in copies:
        copy.wait()


def polar_part(recv, high, low, weights, slots, cols):
    tiles, _, channels = recv.shape
    vmem = pl.BlockSpec(memory_space=pltpu.VMEM)
    shape = (slots, tiles * cols, channels)
    return pl.pallas_call(
        functools.partial(polar_kernel, slots, cols),
        out_shape=jax.ShapeDtypeStruct(shape, BF16),
        in_specs=[vmem] * 7,
        out_specs=pl.BlockSpec(memory_space=pltpu.HBM),
        scratch_shapes=[
            pltpu.VMEM((slots, tiles * cols + 32, channels), BF16),
            pltpu.VMEM(shape, BF16),
            pltpu.SemaphoreType.DMA((slots,)),
        ],
        compiler_params=pltpu.CompilerParams(vmem_limit_bytes=VMEM_BYTES),
        cost_estimate=pl.CostEstimate(flops=6 * 10**8, bytes_accessed=2 * 10**6, transcendentals=10**6),
        name="polar",
    )(recv, high, low, *weights)


def body(
    field,
    land_mask,
    zonal_tap_weight,
    norm_gain,
    up_weight,
    down_weight,
    polar_rows,
    polar_owner,
    polar_taps,
):
    lat_rows, cols, channels = field.shape
    tiles = lax.axis_size("lon")
    slots = max(2, lat_rows // tiles)
    weights = (
        zonal_tap_weight,
        norm_gain.reshape(1, channels),
        up_weight,
        down_weight,
    )
    masked, outgoing = prep(field, land_mask, polar_rows, polar_owner, tiles, slots)
    swap_pairs = [(i, i ^ 1) for i in range(tiles)]
    cross_pairs = [(i, (i + 1) % tiles if i % 2 else (i - 1) % tiles) for i in range(tiles)]
    cross = lax.ppermute(masked, "lon", cross_pairs)
    swap = lax.ppermute(masked, "lon", swap_pairs)
    recv = lax.all_to_all(outgoing, "lon", split_axis=0, concat_axis=0, tiled=True)
    mixed, high, low = tile_part(polar_taps, masked, cross, swap, land_mask, weights)
    polar = polar_part(recv, high, low, weights, slots, cols)
    return (mixed, polar)


def solution(mesh):
    in_specs = (P("lat", "lon", None), P("lat", "lon"), P(), P(), P(), P(), P("lat"), P("lat"), P())
    out_specs = (P("lat", "lon", None), P(("lat", "lon"), None, None))
    return jax.shard_map(body, mesh=mesh, in_specs=in_specs, out_specs=out_specs, check_vma=False)
```

```python
import functools

import jax
import jax.numpy as jnp
from jax import lax
from jax.experimental import pallas as pl
from jax.experimental.pallas import tpu as pltpu
from jax.sharding import PartitionSpec as P

DILATION_STEP = 4
EXTRA = 16
PARTS = 1
SHARES = 2
VMEM_BYTES = 48 * 1024 * 1024
F32 = jnp.float32
BF16 = jnp.bfloat16


def spread_mask(mask_rows, channels):
    n, cols = mask_rows.shape
    eye = (
        lax.broadcasted_iota(jnp.int32, (cols, cols), 0)
        == lax.broadcasted_iota(jnp.int32, (cols, cols), 1)
    ).astype(F32)
    picked = (mask_rows[:, None, :] * eye[None]).astype(BF16).reshape(n * cols, cols)
    return jnp.dot(picked, jnp.ones((cols, channels), BF16), preferred_element_type=F32)


def branch_rows(triples, taps, gain, up, down):
    zonal = []
    n_taps = len(taps)
    for left, own, right in triples:
        cols = own.shape[0]
        start = cols - n_taps // 2 * DILATION_STEP
        line = jnp.concatenate([left, own, right], axis=0).astype(F32)
        aligned = shifted = None
        for k in range(n_taps):
            at = start + k * DILATION_STEP
            if at % 8 == 0:
                term = line[at : at + cols] * taps[k]
                aligned = term if aligned is None else aligned + term
            else:
                term = line[at - 4 : at - 4 + cols + 8] * taps[k]
                shifted = term if shifted is None else shifted + term
        zonal.append(aligned + shifted[4 : 4 + cols])
    zonal = jnp.concatenate(zonal, axis=0)
    mean = jnp.mean(zonal, axis=-1, keepdims=True)
    centred = zonal - mean
    var = jnp.mean(centred * centred, axis=-1, keepdims=True)
    normed = (centred * lax.rsqrt(var + 1e-6) * gain).astype(BF16)
    pre = jnp.dot(normed, up, preferred_element_type=F32)
    inner = pre * (0.7978845608028654 + (0.7978845608028654 * 0.044715) * (pre * pre))
    twice = (pre + pre * jnp.tanh(inner)).astype(BF16)
    return jnp.dot(twice, down, preferred_element_type=F32) * 0.5


def prep_kernel(
    slots, rows_hbm, owner_hbm, field_hbm, mask_hbm, masked_hbm, out_hbm,
    rows, owners, count, field, masked, mask_t, mask_f, extra, extra_half, small_sems, load_sems, store_sems, row_sems, extra_sem,
):
    lat_rows, cols, channels = field.shape
    tiles = out_hbm.shape[0]
    parts = load_sems.shape[0]
    some = lat_rows // parts
    entries = owners.shape[0]
    small = [
        pltpu.make_async_copy(rows_hbm, rows, small_sems.at[0]),
        pltpu.make_async_copy(owner_hbm, owners, small_sems.at[1]),
        pltpu.make_async_copy(mask_hbm, mask_t, small_sems.at[2]),
    ]
    blocks = [pl.ds(p * some, some) for p in range(parts)]
    loads = [pltpu.make_async_copy(field_hbm.at[b], field.at[b], load_sems.at[p]) for p, b in enumerate(blocks)]
    stores = [pltpu.make_async_copy(masked.at[b], masked_hbm.at[b], store_sems.at[p]) for p, b in enumerate(blocks)]
    for copy in small + loads:
        copy.start()
    mask_f[...] = jnp.zeros_like(mask_f)
    extra[...] = jnp.zeros_like(extra)
    for tile in range(tiles):
        count[tile] = 0

    def row_copy(e, row, owner, rank):
        return pltpu.make_async_copy(
            masked.at[row],
            out_hbm.at[owner, pl.ds(pl.multiple_of(rank * cols, cols), cols)],
            row_sems.at[e],
        )

    for copy in small:
        copy.wait()
    mask = mask_t[...].astype(F32).T
    mask_f[:, :cols] = mask
    places = []
    for e in range(entries):
        owner = owners[e]
        row = rows[e]
        rank = count[owner]
        count[owner] = rank + 1
        extra[pl.ds(owner * EXTRA + rank, 1), :] = mask_f[pl.ds(row, 1), :]
        places.append((row, owner, rank))
    extra_half[...] = extra[...].astype(BF16).reshape(tiles, EXTRA, channels)
    extra_copy = pltpu.make_async_copy(extra_half, out_hbm.at[:, pl.ds(slots * cols, EXTRA)], extra_sem)
    extra_copy.start()
    for p in range(parts):
        at = slice(p * some, (p + 1) * some)
        wide = spread_mask(mask[at], channels).astype(BF16)
        loads[p].wait()
        masked[at] = field[at] * wide.reshape(some, cols, channels)
        stores[p].start()
    for e, place in enumerate(places):
        row_copy(e, *place).start()
    for e, place in enumerate(places):
        row_copy(e, *place).wait()
    extra_copy.wait()
    for store in stores:
        store.wait()


def prep(field, land_mask, polar_rows, polar_owner, tiles, slots):
    lat_rows, cols, channels = field.shape
    hbm = pl.BlockSpec(memory_space=pltpu.HBM)
    return pl.pallas_call(
        functools.partial(prep_kernel, slots),
        out_shape=(
            jax.ShapeDtypeStruct(field.shape, BF16),
            jax.ShapeDtypeStruct((tiles, slots * cols + EXTRA, channels), BF16),
        ),
        in_specs=[hbm] * 4,
        out_specs=(hbm, hbm),
        scratch_shapes=[
            pltpu.SMEM(polar_rows.shape, jnp.int32),
            pltpu.SMEM(polar_owner.shape, jnp.int32),
            pltpu.SMEM((tiles,), jnp.int32),
            pltpu.VMEM(field.shape, BF16),
            pltpu.VMEM(field.shape, BF16),
            pltpu.VMEM((cols, lat_rows), jnp.int32),
            pltpu.VMEM((lat_rows, channels), F32),
            pltpu.VMEM((tiles * EXTRA, channels), F32),
            pltpu.VMEM((tiles, EXTRA, channels), BF16),
            pltpu.SemaphoreType.DMA((3,)),
            pltpu.SemaphoreType.DMA((PARTS,)),
            pltpu.SemaphoreType.DMA((PARTS,)),
            pltpu.SemaphoreType.DMA(polar_owner.shape),
            pltpu.SemaphoreType.DMA,
        ],
        cost_estimate=pl.CostEstimate(flops=10**6, bytes_accessed=2 * 10**6, transcendentals=0),
        name="prep",
    )(polar_rows, polar_owner, field, land_mask.T)


def tile_kernel(
    chunk, polar_taps_ref, own_ref, cross_ref, swap_ref, mask_ref, taps_ref, gain_ref, up_ref, down_ref,
    mixed_ref, bands_ref, left, right, mask_f,
):
    lat_rows, cols, channels = own_ref.shape
    me = lax.axis_index("lon")
    odd = lax.rem(me, 2)

    @pl.when(odd == 0)
    def _():
        left[...] = cross_ref[...]
        right[...] = swap_ref[...]

    @pl.when(odd == 1)
    def _():
        left[...] = swap_ref[...]
        right[...] = cross_ref[...]

    mask_f[...] = mask_ref[...].astype(F32).T

    def some_rows(step, _):
        at = pl.ds(step * chunk, chunk)
        triples = [(left[step * chunk + r], own_ref[step * chunk + r], right[step * chunk + r]) for r in range(chunk)]
        taps = [taps_ref[k : k + 1] for k in range(taps_ref.shape[0])]
        branch = branch_rows(triples, taps, gain_ref[...], up_ref[...], down_ref[...])
        wide = spread_mask(mask_f[at, :], channels)
        own = own_ref[at].reshape(chunk * cols, channels).astype(F32)
        mixed = wide * (own + branch.astype(BF16).astype(F32))
        mixed_ref[at] = mixed.astype(BF16).reshape(chunk, cols, channels)
        return 0

    lax.fori_loop(0, lat_rows // chunk, some_rows, 0)

    n, depth = bands_ref.shape[0] // 2, bands_ref.shape[1]
    n_taps = polar_taps_ref.shape[0]
    offset = lax.broadcasted_iota(jnp.int32, (n, depth), 1) - lax.broadcasted_iota(jnp.int32, (n, depth), 0)
    first = (depth - n) // 2 - n_taps // 2
    band = jnp.zeros((n, depth), F32)
    for k in range(n_taps):
        band = jnp.where(offset == k + first, polar_taps_ref[k], band)
    high = band.astype(BF16)
    bands_ref[:n] = high
    bands_ref[n:] = (band - high.astype(F32)).astype(BF16)


def tile_part(polar_taps, masked, cross, swap, land_mask, weights):
    lat_rows, cols, channels = masked.shape
    smem = pl.BlockSpec(memory_space=pltpu.SMEM)
    vmem = pl.BlockSpec(memory_space=pltpu.VMEM)
    return pl.pallas_call(
        functools.partial(tile_kernel, 32),
        out_shape=(
            jax.ShapeDtypeStruct(masked.shape, BF16),
            jax.ShapeDtypeStruct((256, 160), BF16),
        ),
        in_specs=[smem] + [vmem] * 8,
        out_specs=(vmem, vmem),
        scratch_shapes=[pltpu.VMEM(masked.shape, BF16)] * 2 + [pltpu.VMEM((lat_rows, cols), F32)],
        compiler_params=pltpu.CompilerParams(vmem_limit_bytes=VMEM_BYTES),
        cost_estimate=pl.CostEstimate(flops=5 * 10**10, bytes_accessed=3 * 10**6, transcendentals=10**6),
        name="tile",
    )(polar_taps, masked, cross, swap, land_mask.T, *weights)


def polar_kernel(
    slots, cols, recv_ref, bands_ref, taps_ref, gain_ref, up_ref, down_ref,
    out_hbm, circle, out, sems,
):
    tiles, _, channels = recv_ref.shape
    n, depth = bands_ref.shape[0] // 2, bands_ref.shape[1]
    pad = (depth - n) // 2
    nlon = tiles * cols
    taps = [taps_ref[k : k + 1] for k in range(taps_ref.shape[0])]
    extra = recv_ref[:, slots * cols :, :].astype(F32)
    copies = []
    share = nlon // n // SHARES
    for pair in range(slots // 2):
        for half in range(2):
            slot = pair * 2 + half
            pieces = [recv_ref[t, slot * cols : (slot + 1) * cols, :].astype(F32) for t in range(tiles)]
            triples = [(pieces[t - 1], pieces[t], pieces[(t + 1) % tiles]) for t in range(tiles)]
            branch = branch_rows(triples, taps, gain_ref[...], up_ref[...], down_ref[...])
            wide = spread_mask(extra[:, slot, :cols], channels)
            own = jnp.concatenate(pieces, axis=0)
            mixed = jnp.where(wide > 0.5, own + branch.astype(BF16).astype(F32), 0.0).astype(BF16)
            lanes = slice(half * channels, (half + 1) * channels)
            circle[pair, pad : nlon + pad, lanes] = mixed
            circle[pair, :pad, lanes] = mixed[nlon - pad :]
            circle[pair, nlon + pad :, lanes] = mixed[:pad]
        for b in range(nlon // n):
            both = jnp.dot(bands_ref[...], circle[pair, b * n : b * n + depth, :], preferred_element_type=F32)
            rows = (both[:n] + both[n:]).astype(BF16)
            for half in range(2):
                out[pair * 2 + half, b * n : (b + 1) * n, :] = rows[:, half * channels : (half + 1) * channels]
            if (b + 1) % share == 0:
                at = (pl.ds(pair * 2, 2), pl.ds((b + 1 - share) * n, share * n))
                copies.append(pltpu.make_async_copy(out.at[at], out_hbm.at[at], sems.at[len(copies)]))
                copies[-1].start()
    for copy in copies:
        copy.wait()


def polar_part(recv, bands, weights, slots, cols):
    tiles, _, channels = recv.shape
    vmem = pl.BlockSpec(memory_space=pltpu.VMEM)
    shape = (slots, tiles * cols, channels)
    return pl.pallas_call(
        functools.partial(polar_kernel, slots, cols),
        out_shape=jax.ShapeDtypeStruct(shape, BF16),
        in_specs=[vmem] * 6,
        out_specs=pl.BlockSpec(memory_space=pltpu.HBM),
        scratch_shapes=[
            pltpu.VMEM((slots // 2, tiles * cols + 32, 2 * channels), BF16),
            pltpu.VMEM(shape, BF16),
            pltpu.SemaphoreType.DMA((slots // 2 * SHARES,)),
        ],
        compiler_params=pltpu.CompilerParams(vmem_limit_bytes=VMEM_BYTES),
        cost_estimate=pl.CostEstimate(flops=6 * 10**8, bytes_accessed=2 * 10**6, transcendentals=10**6),
        name="polar",
    )(recv, bands, *weights)


def body(
    field,
    land_mask,
    zonal_tap_weight,
    norm_gain,
    up_weight,
    down_weight,
    polar_rows,
    polar_owner,
    polar_taps,
):
    lat_rows, cols, channels = field.shape
    tiles = lax.axis_size("lon")
    slots = max(2, lat_rows // tiles)
    weights = (
        zonal_tap_weight,
        norm_gain.reshape(1, channels),
        up_weight,
        down_weight,
    )
    masked, outgoing = prep(field, land_mask, polar_rows, polar_owner, tiles, slots)
    swap_pairs = [(i, i ^ 1) for i in range(tiles)]
    cross_pairs = [(i, (i + 1) % tiles if i % 2 else (i - 1) % tiles) for i in range(tiles)]
    cross = lax.ppermute(masked, "lon", cross_pairs)
    swap = lax.ppermute(masked, "lon", swap_pairs)
    recv = lax.all_to_all(outgoing, "lon", split_axis=0, concat_axis=0, tiled=True)
    mixed, bands = tile_part(polar_taps, masked, cross, swap, land_mask, weights)
    polar = polar_part(recv, bands, weights, slots, cols)
    return (mixed, polar)


def solution(mesh):
    in_specs = (P("lat", "lon", None), P("lat", "lon"), P(), P(), P(), P(), P("lat"), P("lat"), P())
    out_specs = (P("lat", "lon", None), P(("lat", "lon"), None, None))
    return jax.shard_map(body, mesh=mesh, in_specs=in_specs, out_specs=out_specs, check_vma=False)
```

```python
import functools

import jax
import jax.numpy as jnp
from jax import lax
from jax.experimental import pallas as pl
from jax.experimental.pallas import tpu as pltpu
from jax.sharding import PartitionSpec as P

DILATION_STEP = 4
EXTRA = 8
TILE_FLOPS = 7 * 10**9
PARTS = 1
SHARES = 2
VMEM_BYTES = 48 * 1024 * 1024
F32 = jnp.float32
BF16 = jnp.bfloat16


def spread_mask(mask_rows, channels):
    n, cols = mask_rows.shape
    eye = (
        lax.broadcasted_iota(jnp.int32, (cols, cols), 0)
        == lax.broadcasted_iota(jnp.int32, (cols, cols), 1)
    ).astype(F32)
    picked = (mask_rows[:, None, :] * eye[None]).astype(BF16).reshape(n * cols, cols)
    return jnp.dot(picked, jnp.ones((cols, channels), BF16), preferred_element_type=F32)


def branch_rows(triples, taps, gain, up, down):
    zonal = []
    n_taps = len(taps)
    for left, own, right in triples:
        cols = own.shape[0]
        start = cols - n_taps // 2 * DILATION_STEP
        line = jnp.concatenate([left, own, right], axis=0).astype(F32)
        aligned = shifted = None
        for k in range(n_taps):
            at = start + k * DILATION_STEP
            if at % 8 == 0:
                term = line[at : at + cols] * taps[k]
                aligned = term if aligned is None else aligned + term
            else:
                term = line[at - 4 : at - 4 + cols + 8] * taps[k]
                shifted = term if shifted is None else shifted + term
        zonal.append(aligned + shifted[4 : 4 + cols])
    zonal = jnp.concatenate(zonal, axis=0)
    mean = jnp.mean(zonal, axis=-1, keepdims=True)
    centred = zonal - mean
    var = jnp.mean(centred * centred, axis=-1, keepdims=True)
    normed = (centred * lax.rsqrt(var + 1e-6) * gain).astype(BF16)
    pre = jnp.dot(normed, up, preferred_element_type=F32)
    inner = pre * (0.7978845608028654 + (0.7978845608028654 * 0.044715) * (pre * pre))
    twice = (pre + pre * jnp.tanh(inner)).astype(BF16)
    return jnp.dot(twice, down, preferred_element_type=F32) * 0.5


def prep_kernel(
    slots, rows_hbm, owner_hbm, field_hbm, mask_hbm, masked_hbm, out_hbm,
    rows, owners, count, field, masked, mask_t, mask_f, extra, extra_half, small_sems, load_sems, store_sems, row_sems, extra_sem,
):
    lat_rows, cols, channels = field.shape
    tiles = out_hbm.shape[0]
    parts = load_sems.shape[0]
    some = lat_rows // parts
    entries = owners.shape[0]
    small = [
        pltpu.make_async_copy(rows_hbm, rows, small_sems.at[0]),
        pltpu.make_async_copy(owner_hbm, owners, small_sems.at[1]),
        pltpu.make_async_copy(mask_hbm, mask_t, small_sems.at[2]),
    ]
    blocks = [pl.ds(p * some, some) for p in range(parts)]
    loads = [pltpu.make_async_copy(field_hbm.at[b], field.at[b], load_sems.at[p]) for p, b in enumerate(blocks)]
    stores = [pltpu.make_async_copy(masked.at[b], masked_hbm.at[b], store_sems.at[p]) for p, b in enumerate(blocks)]
    for copy in small + loads:
        copy.start()
    mask_f[...] = jnp.zeros_like(mask_f)
    extra[...] = jnp.zeros_like(extra)
    for tile in range(tiles):
        count[tile] = 0

    def row_copy(e, row, owner, rank):
        return pltpu.make_async_copy(
            masked.at[row],
            out_hbm.at[owner, pl.ds(pl.multiple_of(rank * cols, cols), cols)],
            row_sems.at[e],
        )

    for copy in small:
        copy.wait()
    mask = mask_t[...].astype(F32).T
    mask_f[:, :cols] = mask
    places = []
    for e in range(entries):
        owner = owners[e]
        row = rows[e]
        rank = count[owner]
        count[owner] = rank + 1
        extra[pl.ds(owner * EXTRA + rank, 1), :] = mask_f[pl.ds(row, 1), :]
        places.append((row, owner, rank))
    extra_half[...] = extra[...].astype(BF16).reshape(tiles, EXTRA, channels)
    extra_copy = pltpu.make_async_copy(extra_half, out_hbm.at[:, pl.ds(slots * cols, EXTRA)], extra_sem)
    extra_copy.start()
    for p in range(parts):
        at = slice(p * some, (p + 1) * some)
        wide = spread_mask(mask[at], channels).astype(BF16)
        loads[p].wait()
        masked[at] = field[at] * wide.reshape(some, cols, channels)
        stores[p].start()
    for e, place in enumerate(places):
        row_copy(e, *place).start()
    for e, place in enumerate(places):
        row_copy(e, *place).wait()
    extra_copy.wait()
    for store in stores:
        store.wait()


def prep(field, land_mask, polar_rows, polar_owner, tiles, slots):
    lat_rows, cols, channels = field.shape
    hbm = pl.BlockSpec(memory_space=pltpu.HBM)
    return pl.pallas_call(
        functools.partial(prep_kernel, slots),
        out_shape=(
            jax.ShapeDtypeStruct(field.shape, BF16),
            jax.ShapeDtypeStruct((tiles, slots * cols + EXTRA, channels), BF16),
        ),
        in_specs=[hbm] * 4,
        out_specs=(hbm, hbm),
        scratch_shapes=[
            pltpu.SMEM(polar_rows.shape, jnp.int32),
            pltpu.SMEM(polar_owner.shape, jnp.int32),
            pltpu.SMEM((tiles,), jnp.int32),
            pltpu.VMEM(field.shape, BF16),
            pltpu.VMEM(field.shape, BF16),
            pltpu.VMEM((cols, lat_rows), jnp.int32),
            pltpu.VMEM((lat_rows, channels), F32),
            pltpu.VMEM((tiles * EXTRA, channels), F32),
            pltpu.VMEM((tiles, EXTRA, channels), BF16),
            pltpu.SemaphoreType.DMA((3,)),
            pltpu.SemaphoreType.DMA((PARTS,)),
            pltpu.SemaphoreType.DMA((PARTS,)),
            pltpu.SemaphoreType.DMA(polar_owner.shape),
            pltpu.SemaphoreType.DMA,
        ],
        cost_estimate=pl.CostEstimate(flops=10**6, bytes_accessed=2 * 10**6, transcendentals=0),
        name="prep",
    )(polar_rows, polar_owner, field, land_mask.T)


def tile_kernel(
    chunk, polar_taps_ref, own_ref, cross_ref, upper_ref, lower_ref, mask_ref, taps_ref, gain_ref, up_ref, down_ref,
    mixed_ref, bands_ref, left, right, mask_f,
):
    lat_rows, cols, channels = own_ref.shape
    half = lat_rows // 2
    odd = lax.rem(lax.axis_index("lon"), 2)

    @pl.when(odd == 0)
    def _():
        left[...] = cross_ref[...]
        right[:half] = upper_ref[...]
        right[half:] = lower_ref[...]

    @pl.when(odd == 1)
    def _():
        left[:half] = upper_ref[...]
        left[half:] = lower_ref[...]
        right[...] = cross_ref[...]

    mask_f[...] = mask_ref[...].astype(F32).T

    def some_rows(step, _):
        at = pl.ds(step * chunk, chunk)
        triples = [(left[step * chunk + r], own_ref[step * chunk + r], right[step * chunk + r]) for r in range(chunk)]
        taps = [taps_ref[k : k + 1] for k in range(taps_ref.shape[0])]
        branch = branch_rows(triples, taps, gain_ref[...], up_ref[...], down_ref[...])
        wide = spread_mask(mask_f[at, :], channels)
        own = own_ref[at].reshape(chunk * cols, channels).astype(F32)
        mixed = wide * (own + branch.astype(BF16).astype(F32))
        mixed_ref[at] = mixed.astype(BF16).reshape(chunk, cols, channels)
        return 0

    lax.fori_loop(0, lat_rows // chunk, some_rows, 0)

    n, depth = bands_ref.shape[0] // 2, bands_ref.shape[1]
    n_taps = polar_taps_ref.shape[0]
    offset = lax.broadcasted_iota(jnp.int32, (n, depth), 1) - lax.broadcasted_iota(jnp.int32, (n, depth), 0)
    first = (depth - n) // 2 - n_taps // 2
    band = jnp.zeros((n, depth), F32)
    for k in range(n_taps):
        band = jnp.where(offset == k + first, polar_taps_ref[k], band)
    high = band.astype(BF16)
    bands_ref[:n] = high
    bands_ref[n:] = (band - high.astype(F32)).astype(BF16)


def tile_part(polar_taps, masked, cross, swaps, land_mask, weights):
    lat_rows, cols, channels = masked.shape
    smem = pl.BlockSpec(memory_space=pltpu.SMEM)
    vmem = pl.BlockSpec(memory_space=pltpu.VMEM)
    return pl.pallas_call(
        functools.partial(tile_kernel, 32),
        out_shape=(
            jax.ShapeDtypeStruct(masked.shape, BF16),
            jax.ShapeDtypeStruct((256, 160), BF16),
        ),
        in_specs=[smem] + [vmem] * 9,
        out_specs=(vmem, vmem),
        scratch_shapes=[pltpu.VMEM(masked.shape, BF16)] * 2 + [pltpu.VMEM((lat_rows, cols), F32)],
        compiler_params=pltpu.CompilerParams(vmem_limit_bytes=VMEM_BYTES),
        cost_estimate=pl.CostEstimate(flops=TILE_FLOPS, bytes_accessed=3 * 10**6, transcendentals=10**6),
        name="tile",
    )(polar_taps, masked, cross, *swaps, land_mask.T, *weights)


def polar_kernel(
    slots, cols, recv_ref, bands_ref, taps_ref, gain_ref, up_ref, down_ref,
    out_hbm, circle, out, sems,
):
    tiles, _, channels = recv_ref.shape
    n, depth = bands_ref.shape[0] // 2, bands_ref.shape[1]
    pad = (depth - n) // 2
    nlon = tiles * cols
    taps = [taps_ref[k : k + 1] for k in range(taps_ref.shape[0])]
    extra = recv_ref[:, slots * cols :, :].astype(F32)
    copies = []
    share = nlon // n // SHARES
    for pair in range(slots // 2):
        for half in range(2):
            slot = pair * 2 + half
            pieces = [recv_ref[t, slot * cols : (slot + 1) * cols, :].astype(F32) for t in range(tiles)]
            triples = [(pieces[t - 1], pieces[t], pieces[(t + 1) % tiles]) for t in range(tiles)]
            branch = branch_rows(triples, taps, gain_ref[...], up_ref[...], down_ref[...])
            wide = spread_mask(extra[:, slot, :cols], channels)
            own = jnp.concatenate(pieces, axis=0)
            mixed = jnp.where(wide > 0.5, own + branch.astype(BF16).astype(F32), 0.0).astype(BF16)
            lanes = slice(half * channels, (half + 1) * channels)
            circle[pair, pad : nlon + pad, lanes] = mixed
            circle[pair, :pad, lanes] = mixed[nlon - pad :]
            circle[pair, nlon + pad :, lanes] = mixed[:pad]
        for b in range(nlon // n):
            both = jnp.dot(bands_ref[...], circle[pair, b * n : b * n + depth, :], preferred_element_type=F32)
            rows = (both[:n] + both[n:]).astype(BF16)
            for half in range(2):
                out[pair * 2 + half, b * n : (b + 1) * n, :] = rows[:, half * channels : (half + 1) * channels]
            if (b + 1) % share == 0:
                at = (pl.ds(pair * 2, 2), pl.ds((b + 1 - share) * n, share * n))
                copies.append(pltpu.make_async_copy(out.at[at], out_hbm.at[at], sems.at[len(copies)]))
                copies[-1].start()
    for copy in copies:
        copy.wait()


def polar_part(recv, bands, weights, slots, cols):
    tiles, _, channels = recv.shape
    vmem = pl.BlockSpec(memory_space=pltpu.VMEM)
    shape = (slots, tiles * cols, channels)
    return pl.pallas_call(
        functools.partial(polar_kernel, slots, cols),
        out_shape=jax.ShapeDtypeStruct(shape, BF16),
        in_specs=[vmem] * 6,
        out_specs=pl.BlockSpec(memory_space=pltpu.HBM),
        scratch_shapes=[
            pltpu.VMEM((slots // 2, tiles * cols + 32, 2 * channels), BF16),
            pltpu.VMEM(shape, BF16),
            pltpu.SemaphoreType.DMA((slots // 2 * SHARES,)),
        ],
        compiler_params=pltpu.CompilerParams(vmem_limit_bytes=VMEM_BYTES),
        cost_estimate=pl.CostEstimate(flops=6 * 10**8, bytes_accessed=2 * 10**6, transcendentals=10**6),
        name="polar",
    )(recv, bands, *weights)


def body(
    field,
    land_mask,
    zonal_tap_weight,
    norm_gain,
    up_weight,
    down_weight,
    polar_rows,
    polar_owner,
    polar_taps,
):
    lat_rows, cols, channels = field.shape
    tiles = lax.axis_size("lon")
    slots = max(2, lat_rows // tiles)
    weights = (
        zonal_tap_weight,
        norm_gain.reshape(1, channels),
        up_weight,
        down_weight,
    )
    masked, outgoing = prep(field, land_mask, polar_rows, polar_owner, tiles, slots)
    swap_pairs = [(i, i ^ 1) for i in range(tiles)]
    cross_pairs = [(i, (i + 1) % tiles if i % 2 else (i - 1) % tiles) for i in range(tiles)]
    cross = lax.ppermute(masked, "lon", cross_pairs)
    half = lat_rows // 2
    swaps = [lax.ppermute(masked[:half], "lon", swap_pairs), lax.ppermute(masked[half:], "lon", swap_pairs)]
    recv = lax.all_to_all(outgoing, "lon", split_axis=0, concat_axis=0, tiled=True)
    mixed, bands = tile_part(polar_taps, masked, cross, swaps, land_mask, weights)
    polar = polar_part(recv, bands, weights, slots, cols)
    return (mixed, polar)


def solution(mesh):
    in_specs = (P("lat", "lon", None), P("lat", "lon"), P(), P(), P(), P(), P("lat"), P("lat"), P())
    out_specs = (P("lat", "lon", None), P(("lat", "lon"), None, None))
    return jax.shard_map(body, mesh=mesh, in_specs=in_specs, out_specs=out_specs, check_vma=False)
```

```python
import functools

import jax
import jax.numpy as jnp
from jax import lax
from jax.experimental import pallas as pl
from jax.experimental.pallas import tpu as pltpu
from jax.sharding import PartitionSpec as P

DILATION_STEP = 4
EXTRA = 8
TILE_FLOPS = 7 * 10**9
PARTS = 1
SHARES = 2
VMEM_BYTES = 48 * 1024 * 1024
PREP_VMEM_BYTES = 62 * 1024 * 1024
F32 = jnp.float32
BF16 = jnp.bfloat16


def spread_mask(mask_rows, channels):
    n, cols = mask_rows.shape
    eye = (
        lax.broadcasted_iota(jnp.int32, (cols, cols), 0)
        == lax.broadcasted_iota(jnp.int32, (cols, cols), 1)
    ).astype(F32)
    picked = (mask_rows[:, None, :] * eye[None]).astype(BF16).reshape(n * cols, cols)
    return jnp.dot(picked, jnp.ones((cols, channels), BF16), preferred_element_type=F32)


def branch_rows(triples, taps, gain, up, down):
    zonal = []
    n_taps = len(taps)
    for left, own, right in triples:
        cols = own.shape[0]
        start = cols - n_taps // 2 * DILATION_STEP
        line = jnp.concatenate([left, own, right], axis=0).astype(F32)
        aligned = shifted = None
        for k in range(n_taps):
            at = start + k * DILATION_STEP
            if at % 8 == 0:
                term = line[at : at + cols] * taps[k]
                aligned = term if aligned is None else aligned + term
            else:
                term = line[at - 4 : at - 4 + cols + 8] * taps[k]
                shifted = term if shifted is None else shifted + term
        zonal.append(aligned + shifted[4 : 4 + cols])
    zonal = jnp.concatenate(zonal, axis=0)
    mean = jnp.mean(zonal, axis=-1, keepdims=True)
    centred = zonal - mean
    var = jnp.mean(centred * centred, axis=-1, keepdims=True)
    normed = (centred * lax.rsqrt(var + 1e-6) * gain).astype(BF16)
    pre = jnp.dot(normed, up, preferred_element_type=F32)
    inner = pre * (0.7978845608028654 + (0.7978845608028654 * 0.044715) * (pre * pre))
    twice = (pre + pre * jnp.tanh(inner)).astype(BF16)
    return jnp.dot(twice, down, preferred_element_type=F32) * 0.5


def prep_kernel(
    slots, rows_hbm, owner_hbm, field_hbm, mask_hbm, masked, out_hbm,
    rows, owners, count, field, mask_t, mask_f, extra, extra_half, small_sems, load_sem, row_sems, extra_sem,
):
    lat_rows, cols, channels = field.shape
    tiles = out_hbm.shape[0]
    entries = owners.shape[0]
    small = [
        pltpu.make_async_copy(rows_hbm, rows, small_sems.at[0]),
        pltpu.make_async_copy(owner_hbm, owners, small_sems.at[1]),
        pltpu.make_async_copy(mask_hbm, mask_t, small_sems.at[2]),
    ]
    load = pltpu.make_async_copy(field_hbm, field, load_sem)
    for copy in small:
        copy.start()
    load.start()
    mask_f[...] = jnp.zeros_like(mask_f)
    extra[...] = jnp.zeros_like(extra)
    for tile in range(tiles):
        count[tile] = 0

    def row_copy(e, row, owner, rank):
        return pltpu.make_async_copy(
            masked.at[row],
            out_hbm.at[owner, pl.ds(pl.multiple_of(rank * cols, cols), cols)],
            row_sems.at[e],
        )

    for copy in small:
        copy.wait()
    mask = mask_t[...].astype(F32).T
    mask_f[:, :cols] = mask
    places = []
    for e in range(entries):
        owner = owners[e]
        row = rows[e]
        rank = count[owner]
        count[owner] = rank + 1
        extra[pl.ds(owner * EXTRA + rank, 1), :] = mask_f[pl.ds(row, 1), :]
        places.append((row, owner, rank))
    extra_half[...] = extra[...].astype(BF16).reshape(tiles, EXTRA, channels)
    extra_copy = pltpu.make_async_copy(extra_half, out_hbm.at[:, pl.ds(slots * cols, EXTRA)], extra_sem)
    extra_copy.start()
    wide = spread_mask(mask, channels).astype(BF16).reshape(lat_rows, cols, channels)
    load.wait()
    masked[...] = field[...] * wide
    for e, place in enumerate(places):
        row_copy(e, *place).start()
    for e, place in enumerate(places):
        row_copy(e, *place).wait()
    extra_copy.wait()


def prep(field, land_mask, polar_rows, polar_owner, tiles, slots):
    lat_rows, cols, channels = field.shape
    hbm = pl.BlockSpec(memory_space=pltpu.HBM)
    vmem = pl.BlockSpec(memory_space=pltpu.VMEM)
    return pl.pallas_call(
        functools.partial(prep_kernel, slots),
        out_shape=(
            pltpu.VMEM(field.shape, BF16),
            jax.ShapeDtypeStruct((tiles, slots * cols + EXTRA, channels), BF16),
        ),
        in_specs=[hbm] * 4,
        out_specs=(vmem, hbm),
        scratch_shapes=[
            pltpu.SMEM(polar_rows.shape, jnp.int32),
            pltpu.SMEM(polar_owner.shape, jnp.int32),
            pltpu.SMEM((tiles,), jnp.int32),
            pltpu.VMEM(field.shape, BF16),
            pltpu.VMEM((cols, lat_rows), jnp.int32),
            pltpu.VMEM((lat_rows, channels), F32),
            pltpu.VMEM((tiles * EXTRA, channels), F32),
            pltpu.VMEM((tiles, EXTRA, channels), BF16),
            pltpu.SemaphoreType.DMA((3,)),
            pltpu.SemaphoreType.DMA,
            pltpu.SemaphoreType.DMA(polar_owner.shape),
            pltpu.SemaphoreType.DMA,
        ],
        compiler_params=pltpu.CompilerParams(vmem_limit_bytes=PREP_VMEM_BYTES),
        cost_estimate=pl.CostEstimate(flops=10**6, bytes_accessed=2 * 10**6, transcendentals=0),
        name="prep",
    )(polar_rows, polar_owner, field, land_mask.T)


def tile_kernel(
    chunk, polar_taps_ref, own_ref, cross_ref, upper_ref, lower_ref, mask_ref, taps_ref, gain_ref, up_ref, down_ref,
    mixed_ref, bands_ref, left, right, mask_f,
):
    lat_rows, cols, channels = own_ref.shape
    half = lat_rows // 2
    odd = lax.rem(lax.axis_index("lon"), 2)

    @pl.when(odd == 0)
    def _():
        left[...] = cross_ref[...]
        right[:half] = upper_ref[...]
        right[half:] = lower_ref[...]

    @pl.when(odd == 1)
    def _():
        left[:half] = upper_ref[...]
        left[half:] = lower_ref[...]
        right[...] = cross_ref[...]

    mask_f[...] = mask_ref[...].astype(F32).T

    def some_rows(step, _):
        at = pl.ds(step * chunk, chunk)
        triples = [(left[step * chunk + r], own_ref[step * chunk + r], right[step * chunk + r]) for r in range(chunk)]
        taps = [taps_ref[k : k + 1] for k in range(taps_ref.shape[0])]
        branch = branch_rows(triples, taps, gain_ref[...], up_ref[...], down_ref[...])
        wide = spread_mask(mask_f[at, :], channels)
        own = own_ref[at].reshape(chunk * cols, channels).astype(F32)
        mixed = wide * (own + branch.astype(BF16).astype(F32))
        mixed_ref[at] = mixed.astype(BF16).reshape(chunk, cols, channels)
        return 0

    lax.fori_loop(0, lat_rows // chunk, some_rows, 0)

    n, depth = bands_ref.shape[0] // 2, bands_ref.shape[1]
    n_taps = polar_taps_ref.shape[0]
    offset = lax.broadcasted_iota(jnp.int32, (n, depth), 1) - lax.broadcasted_iota(jnp.int32, (n, depth), 0)
    first = (depth - n) // 2 - n_taps // 2
    band = jnp.zeros((n, depth), F32)
    for k in range(n_taps):
        band = jnp.where(offset == k + first, polar_taps_ref[k], band)
    high = band.astype(BF16)
    bands_ref[:n] = high
    bands_ref[n:] = (band - high.astype(F32)).astype(BF16)


def tile_part(polar_taps, masked, cross, swaps, land_mask, weights):
    lat_rows, cols, channels = masked.shape
    smem = pl.BlockSpec(memory_space=pltpu.SMEM)
    vmem = pl.BlockSpec(memory_space=pltpu.VMEM)
    return pl.pallas_call(
        functools.partial(tile_kernel, 32),
        out_shape=(
            jax.ShapeDtypeStruct(masked.shape, BF16),
            jax.ShapeDtypeStruct((256, 160), BF16),
        ),
        in_specs=[smem] + [vmem] * 9,
        out_specs=(vmem, vmem),
        scratch_shapes=[pltpu.VMEM(masked.shape, BF16)] * 2 + [pltpu.VMEM((lat_rows, cols), F32)],
        compiler_params=pltpu.CompilerParams(vmem_limit_bytes=VMEM_BYTES),
        cost_estimate=pl.CostEstimate(flops=TILE_FLOPS, bytes_accessed=3 * 10**6, transcendentals=10**6),
        name="tile",
    )(polar_taps, masked, cross, *swaps, land_mask.T, *weights)


def polar_kernel(
    slots, cols, recv_ref, bands_ref, taps_ref, gain_ref, up_ref, down_ref,
    out_hbm, circle, out, sems,
):
    tiles, _, channels = recv_ref.shape
    n, depth = bands_ref.shape[0] // 2, bands_ref.shape[1]
    pad = (depth - n) // 2
    nlon = tiles * cols
    taps = [taps_ref[k : k + 1] for k in range(taps_ref.shape[0])]
    extra = recv_ref[:, slots * cols :, :].astype(F32)
    copies = []
    share = nlon // n // SHARES
    for pair in range(slots // 2):
        for half in range(2):
            slot = pair * 2 + half
            pieces = [recv_ref[t, slot * cols : (slot + 1) * cols, :].astype(F32) for t in range(tiles)]
            triples = [(pieces[t - 1], pieces[t], pieces[(t + 1) % tiles]) for t in range(tiles)]
            branch = branch_rows(triples, taps, gain_ref[...], up_ref[...], down_ref[...])
            wide = spread_mask(extra[:, slot, :cols], channels)
            own = jnp.concatenate(pieces, axis=0)
            mixed = jnp.where(wide > 0.5, own + branch.astype(BF16).astype(F32), 0.0).astype(BF16)
            lanes = slice(half * channels, (half + 1) * channels)
            circle[pair, pad : nlon + pad, lanes] = mixed
            circle[pair, :pad, lanes] = mixed[nlon - pad :]
            circle[pair, nlon + pad :, lanes] = mixed[:pad]
        for b in range(nlon // n):
            both = jnp.dot(bands_ref[...], circle[pair, b * n : b * n + depth, :], preferred_element_type=F32)
            rows = (both[:n] + both[n:]).astype(BF16)
            for half in range(2):
                out[pair * 2 + half, b * n : (b + 1) * n, :] = rows[:, half * channels : (half + 1) * channels]
            if (b + 1) % share == 0:
                at = (pl.ds(pair * 2, 2), pl.ds((b + 1 - share) * n, share * n))
                copies.append(pltpu.make_async_copy(out.at[at], out_hbm.at[at], sems.at[len(copies)]))
                copies[-1].start()
    for copy in copies:
        copy.wait()


def polar_part(recv, bands, weights, slots, cols):
    tiles, _, channels = recv.shape
    vmem = pl.BlockSpec(memory_space=pltpu.VMEM)
    shape = (slots, tiles * cols, channels)
    return pl.pallas_call(
        functools.partial(polar_kernel, slots, cols),
        out_shape=jax.ShapeDtypeStruct(shape, BF16),
        in_specs=[vmem] * 6,
        out_specs=pl.BlockSpec(memory_space=pltpu.HBM),
        scratch_shapes=[
            pltpu.VMEM((slots // 2, tiles * cols + 32, 2 * channels), BF16),
            pltpu.VMEM(shape, BF16),
            pltpu.SemaphoreType.DMA((slots // 2 * SHARES,)),
        ],
        compiler_params=pltpu.CompilerParams(vmem_limit_bytes=VMEM_BYTES),
        cost_estimate=pl.CostEstimate(flops=6 * 10**8, bytes_accessed=2 * 10**6, transcendentals=10**6),
        name="polar",
    )(recv, bands, *weights)


def body(
    field,
    land_mask,
    zonal_tap_weight,
    norm_gain,
    up_weight,
    down_weight,
    polar_rows,
    polar_owner,
    polar_taps,
):
    lat_rows, cols, channels = field.shape
    tiles = lax.axis_size("lon")
    slots = max(2, lat_rows // tiles)
    weights = (
        zonal_tap_weight,
        norm_gain.reshape(1, channels),
        up_weight,
        down_weight,
    )
    masked, outgoing = prep(field, land_mask, polar_rows, polar_owner, tiles, slots)
    swap_pairs = [(i, i ^ 1) for i in range(tiles)]
    cross_pairs = [(i, (i + 1) % tiles if i % 2 else (i - 1) % tiles) for i in range(tiles)]
    cross = lax.ppermute(masked, "lon", cross_pairs)
    half = lat_rows // 2
    swaps = [lax.ppermute(masked[:half], "lon", swap_pairs), lax.ppermute(masked[half:], "lon", swap_pairs)]
    recv = lax.all_to_all(outgoing, "lon", split_axis=0, concat_axis=0, tiled=True)
    mixed, bands = tile_part(polar_taps, masked, cross, swaps, land_mask, weights)
    polar = polar_part(recv, bands, weights, slots, cols)
    return (mixed, polar)


def solution(mesh):
    in_specs = (P("lat", "lon", None), P("lat", "lon"), P(), P(), P(), P(), P("lat"), P("lat"), P())
    out_specs = (P("lat", "lon", None), P(("lat", "lon"), None, None))
    return jax.shard_map(body, mesh=mesh, in_specs=in_specs, out_specs=out_specs, check_vma=False)
```

```python
import functools

import jax
import jax.numpy as jnp
from jax import lax
from jax.experimental import pallas as pl
from jax.experimental.pallas import tpu as pltpu
from jax.sharding import PartitionSpec as P

DILATION_STEP = 4
EXTRA = 8
TILE_FLOPS = 7 * 10**9
PARTS = 1
SHARES = 2
VMEM_BYTES = 48 * 1024 * 1024
PREP_VMEM_BYTES = 62 * 1024 * 1024
F32 = jnp.float32
BF16 = jnp.bfloat16


def spread_mask(mask_rows, channels):
    n, cols = mask_rows.shape
    eye = (
        lax.broadcasted_iota(jnp.int32, (cols, cols), 0)
        == lax.broadcasted_iota(jnp.int32, (cols, cols), 1)
    ).astype(F32)
    picked = (mask_rows[:, None, :] * eye[None]).astype(BF16).reshape(n * cols, cols)
    return jnp.dot(picked, jnp.ones((cols, channels), BF16), preferred_element_type=F32)


def branch_rows(triples, table, up, down):
    zonal = []
    n_taps = table.shape[0] - 1
    taps = [table[k : k + 1] for k in range(n_taps)]
    gain = table[n_taps:]
    for left, own, right in triples:
        cols = own.shape[0]
        start = cols - n_taps // 2 * DILATION_STEP
        line = jnp.concatenate([left, own, right], axis=0).astype(F32)
        aligned = shifted = None
        for k in range(n_taps):
            at = start + k * DILATION_STEP
            if at % 8 == 0:
                term = line[at : at + cols] * taps[k]
                aligned = term if aligned is None else aligned + term
            else:
                term = line[at - 4 : at - 4 + cols + 8] * taps[k]
                shifted = term if shifted is None else shifted + term
        zonal.append(aligned + shifted[4 : 4 + cols])
    zonal = jnp.concatenate(zonal, axis=0)
    mean = jnp.mean(zonal, axis=-1, keepdims=True)
    centred = zonal - mean
    var = jnp.mean(centred * centred, axis=-1, keepdims=True)
    normed = (centred * lax.rsqrt(var + 1e-6) * gain).astype(BF16)
    pre = jnp.dot(normed, up, preferred_element_type=F32)
    inner = pre * (0.7978845608028654 + (0.7978845608028654 * 0.044715) * (pre * pre))
    twice = (pre + pre * jnp.tanh(inner)).astype(BF16)
    return jnp.dot(twice, down, preferred_element_type=F32) * 0.5


def prep_kernel(
    slots, rows_hbm, owner_hbm, field_hbm, mask_hbm, masked, out_hbm,
    rows, owners, count, field, mask_t, mask_f, extra, extra_half, small_sems, load_sem, row_sems, extra_sem,
):
    lat_rows, cols, channels = field.shape
    tiles = out_hbm.shape[0]
    entries = owners.shape[0]
    small = [
        pltpu.make_async_copy(rows_hbm, rows, small_sems.at[0]),
        pltpu.make_async_copy(owner_hbm, owners, small_sems.at[1]),
        pltpu.make_async_copy(mask_hbm, mask_t, small_sems.at[2]),
    ]
    load = pltpu.make_async_copy(field_hbm, field, load_sem)
    for copy in small:
        copy.start()
    load.start()
    mask_f[...] = jnp.zeros_like(mask_f)
    extra[...] = jnp.zeros_like(extra)
    for tile in range(tiles):
        count[tile] = 0

    def row_copy(e, row, owner, rank):
        return pltpu.make_async_copy(
            masked.at[row],
            out_hbm.at[owner, pl.ds(pl.multiple_of(rank * cols, cols), cols)],
            row_sems.at[e],
        )

    for copy in small:
        copy.wait()
    mask = mask_t[...].astype(F32).T
    mask_f[:, :cols] = mask
    places = []
    for e in range(entries):
        owner = owners[e]
        row = rows[e]
        rank = count[owner]
        count[owner] = rank + 1
        extra[pl.ds(owner * EXTRA + rank, 1), :] = mask_f[pl.ds(row, 1), :]
        places.append((row, owner, rank))
    extra_half[...] = extra[...].astype(BF16).reshape(tiles, EXTRA, channels)
    extra_copy = pltpu.make_async_copy(extra_half, out_hbm.at[:, pl.ds(slots * cols, EXTRA)], extra_sem)
    extra_copy.start()
    wide = spread_mask(mask, channels).astype(BF16).reshape(lat_rows, cols, channels)
    load.wait()
    masked[...] = field[...] * wide
    for e, place in enumerate(places):
        row_copy(e, *place).start()
    for e, place in enumerate(places):
        row_copy(e, *place).wait()
    extra_copy.wait()


def prep(field, land_mask, polar_rows, polar_owner, tiles, slots):
    lat_rows, cols, channels = field.shape
    hbm = pl.BlockSpec(memory_space=pltpu.HBM)
    vmem = pl.BlockSpec(memory_space=pltpu.VMEM)
    return pl.pallas_call(
        functools.partial(prep_kernel, slots),
        out_shape=(
            pltpu.VMEM(field.shape, BF16),
            jax.ShapeDtypeStruct((tiles, slots * cols + EXTRA, channels), BF16),
        ),
        in_specs=[hbm] * 4,
        out_specs=(vmem, hbm),
        scratch_shapes=[
            pltpu.SMEM(polar_rows.shape, jnp.int32),
            pltpu.SMEM(polar_owner.shape, jnp.int32),
            pltpu.SMEM((tiles,), jnp.int32),
            pltpu.VMEM(field.shape, BF16),
            pltpu.VMEM((cols, lat_rows), jnp.int32),
            pltpu.VMEM((lat_rows, channels), F32),
            pltpu.VMEM((tiles * EXTRA, channels), F32),
            pltpu.VMEM((tiles, EXTRA, channels), BF16),
            pltpu.SemaphoreType.DMA((3,)),
            pltpu.SemaphoreType.DMA,
            pltpu.SemaphoreType.DMA(polar_owner.shape),
            pltpu.SemaphoreType.DMA,
        ],
        compiler_params=pltpu.CompilerParams(vmem_limit_bytes=PREP_VMEM_BYTES),
        cost_estimate=pl.CostEstimate(flops=10**6, bytes_accessed=2 * 10**6, transcendentals=0),
        name="prep",
    )(polar_rows, polar_owner, field, land_mask.T)


def side_kernel(polar_taps_ref, mask_ref, upper_ref, lower_ref, taps_ref, gain_ref, mask_f, near, table, bands_ref):
    half = upper_ref.shape[0]
    mask_f[...] = mask_ref[...].astype(F32).T
    near[:half] = upper_ref[...]
    near[half:] = lower_ref[...]
    table[: taps_ref.shape[0]] = taps_ref[...]
    table[taps_ref.shape[0] :] = gain_ref[...]
    n, depth = bands_ref.shape[0] // 2, bands_ref.shape[1]
    n_taps = polar_taps_ref.shape[0]
    offset = lax.broadcasted_iota(jnp.int32, (n, depth), 1) - lax.broadcasted_iota(jnp.int32, (n, depth), 0)
    first = (depth - n) // 2 - n_taps // 2
    band = jnp.zeros((n, depth), F32)
    for k in range(n_taps):
        band = jnp.where(offset == k + first, polar_taps_ref[k], band)
    high = band.astype(BF16)
    bands_ref[:n] = high
    bands_ref[n:] = (band - high.astype(F32)).astype(BF16)


def side_part(polar_taps, land_mask, swaps, zonal_tap_weight, norm_gain):
    lat_rows, cols = land_mask.shape
    smem = pl.BlockSpec(memory_space=pltpu.SMEM)
    vmem = pl.BlockSpec(memory_space=pltpu.VMEM)
    half, _, channels = swaps[0].shape
    return pl.pallas_call(
        side_kernel,
        out_shape=(
            jax.ShapeDtypeStruct((lat_rows, cols), F32),
            jax.ShapeDtypeStruct((2 * half, cols, channels), BF16),
            jax.ShapeDtypeStruct((zonal_tap_weight.shape[0] + 1, channels), F32),
            jax.ShapeDtypeStruct((256, 160), BF16),
        ),
        in_specs=[smem] + [vmem] * 5,
        out_specs=(vmem,) * 4,
        compiler_params=pltpu.CompilerParams(vmem_limit_bytes=VMEM_BYTES),
        cost_estimate=pl.CostEstimate(flops=10**6, bytes_accessed=10**6, transcendentals=0),
        name="side",
    )(polar_taps, land_mask.T, *swaps, zonal_tap_weight, norm_gain.reshape(1, channels))


def tile_kernel(own_ref, cross_ref, near_ref, mask_ref, table_ref, up_ref, down_ref, mixed_ref):
    lat_rows, cols, channels = own_ref.shape
    odd = lax.rem(lax.axis_index("lon"), 2)

    def all_rows(left, right):
        triples = [(left[r], own_ref[r], right[r]) for r in range(lat_rows)]
        branch = branch_rows(triples, table_ref[...], up_ref[...], down_ref[...])
        wide = spread_mask(mask_ref[...], channels)
        own = own_ref[...].reshape(lat_rows * cols, channels).astype(F32)
        mixed = wide * (own + branch.astype(BF16).astype(F32))
        mixed_ref[...] = mixed.astype(BF16).reshape(lat_rows, cols, channels)

    pl.when(odd == 0)(functools.partial(all_rows, cross_ref, near_ref))
    pl.when(odd == 1)(functools.partial(all_rows, near_ref, cross_ref))


def tile_part(masked, cross, near, mask_f, weights):
    vmem = pl.BlockSpec(memory_space=pltpu.VMEM)
    return pl.pallas_call(
        tile_kernel,
        out_shape=jax.ShapeDtypeStruct(masked.shape, BF16),
        in_specs=[vmem] * 7,
        out_specs=vmem,
        compiler_params=pltpu.CompilerParams(vmem_limit_bytes=VMEM_BYTES),
        cost_estimate=pl.CostEstimate(flops=TILE_FLOPS, bytes_accessed=3 * 10**6, transcendentals=10**6),
        name="tile",
    )(masked, cross, near, mask_f, *weights)


def polar_kernel(
    slots, cols, recv_ref, bands_ref, table_ref, up_ref, down_ref,
    out_hbm, circle, out, sems,
):
    tiles, _, channels = recv_ref.shape
    n, depth = bands_ref.shape[0] // 2, bands_ref.shape[1]
    pad = (depth - n) // 2
    nlon = tiles * cols
    extra = recv_ref[:, slots * cols :, :].astype(F32)
    share = nlon // n // SHARES

    def out_copy(pair, part):
        at = (pl.ds(pair * 2, 2), pl.ds(part * share * n, share * n))
        return pltpu.make_async_copy(out.at[at], out_hbm.at[at], sems.at[pair, part])

    def filter_pair(pair):
        for half in range(2):
            slot = pair * 2 + half
            pieces = [recv_ref[t, slot * cols : (slot + 1) * cols, :].astype(F32) for t in range(tiles)]
            triples = [(pieces[t - 1], pieces[t], pieces[(t + 1) % tiles]) for t in range(tiles)]
            branch = branch_rows(triples, table_ref[...], up_ref[...], down_ref[...])
            wide = spread_mask(extra[:, slot, :cols], channels)
            own = jnp.concatenate(pieces, axis=0)
            mixed = jnp.where(wide > 0.5, own + branch.astype(BF16).astype(F32), 0.0).astype(BF16)
            lanes = slice(half * channels, (half + 1) * channels)
            circle[pair, pad : nlon + pad, lanes] = mixed
            circle[pair, :pad, lanes] = mixed[nlon - pad :]
            circle[pair, nlon + pad :, lanes] = mixed[:pad]
        for b in range(nlon // n):
            both = jnp.dot(bands_ref[...], circle[pair, b * n : b * n + depth, :], preferred_element_type=F32)
            rows = (both[:n] + both[n:]).astype(BF16)
            for half in range(2):
                out[pair * 2 + half, b * n : (b + 1) * n, :] = rows[:, half * channels : (half + 1) * channels]
            if (b + 1) % share == 0:
                out_copy(pair, b // share).start()

    def clear_pair(pair):
        out[pair * 2 : pair * 2 + 2] = jnp.zeros_like(out[pair * 2 : pair * 2 + 2])
        for part in range(SHARES):
            out_copy(pair, part).start()

    pairs = slots // 2

    def all_pairs():
        for pair in range(pairs):
            filter_pair(pair)

    def first_pair():
        for pair in range(1, pairs):
            clear_pair(pair)
        filter_pair(0)

    if pairs > 1:
        ocean = jnp.max(extra[:, 2:slots, :])
        pl.when(ocean > 0.5)(all_pairs)
        pl.when(jnp.logical_not(ocean > 0.5))(first_pair)
    else:
        all_pairs()
    for pair in range(pairs):
        for part in range(SHARES):
            out_copy(pair, part).wait()


def polar_part(recv, bands, weights, slots, cols):
    tiles, _, channels = recv.shape
    vmem = pl.BlockSpec(memory_space=pltpu.VMEM)
    shape = (slots, tiles * cols, channels)
    return pl.pallas_call(
        functools.partial(polar_kernel, slots, cols),
        out_shape=jax.ShapeDtypeStruct(shape, BF16),
        in_specs=[vmem] * 5,
        out_specs=pl.BlockSpec(memory_space=pltpu.HBM),
        scratch_shapes=[
            pltpu.VMEM((slots // 2, tiles * cols + 32, 2 * channels), BF16),
            pltpu.VMEM(shape, BF16),
            pltpu.SemaphoreType.DMA((slots // 2, SHARES)),
        ],
        compiler_params=pltpu.CompilerParams(vmem_limit_bytes=VMEM_BYTES),
        cost_estimate=pl.CostEstimate(flops=6 * 10**8, bytes_accessed=2 * 10**6, transcendentals=10**6),
        name="polar",
    )(recv, bands, *weights)


def body(
    field,
    land_mask,
    zonal_tap_weight,
    norm_gain,
    up_weight,
    down_weight,
    polar_rows,
    polar_owner,
    polar_taps,
):
    lat_rows, cols, channels = field.shape
    tiles = lax.axis_size("lon")
    slots = max(2, lat_rows // tiles)
    masked, outgoing = prep(field, land_mask, polar_rows, polar_owner, tiles, slots)
    swap_pairs = [(i, i ^ 1) for i in range(tiles)]
    cross_pairs = [(i, (i + 1) % tiles if i % 2 else (i - 1) % tiles) for i in range(tiles)]
    cross = lax.ppermute(masked, "lon", cross_pairs)
    half = lat_rows // 2
    swaps = [lax.ppermute(masked[:half], "lon", swap_pairs), lax.ppermute(masked[half:], "lon", swap_pairs)]
    recv = lax.all_to_all(outgoing, "lon", split_axis=0, concat_axis=0, tiled=True)
    mask_f, near, table, bands = side_part(polar_taps, land_mask, swaps, zonal_tap_weight, norm_gain)
    weights = (table, up_weight, down_weight)
    mixed = tile_part(masked, cross, near, mask_f, weights)
    polar = polar_part(recv, bands, weights, slots, cols)
    return (mixed, polar)


def solution(mesh):
    in_specs = (P("lat", "lon", None), P("lat", "lon"), P(), P(), P(), P(), P("lat"), P("lat"), P())
    out_specs = (P("lat", "lon", None), P(("lat", "lon"), None, None))
    return jax.shard_map(body, mesh=mesh, in_specs=in_specs, out_specs=out_specs, check_vma=False)
```

```python
import functools

import jax
import jax.numpy as jnp
from jax import lax
from jax.experimental import pallas as pl
from jax.experimental.pallas import tpu as pltpu
from jax.sharding import PartitionSpec as P

DILATION_STEP = 4
EXTRA = 8
TILE_FLOPS = 7 * 10**9
PARTS = 1
SHARES = 2
VMEM_BYTES = 48 * 1024 * 1024
PREP_VMEM_BYTES = 62 * 1024 * 1024
F32 = jnp.float32
BF16 = jnp.bfloat16


def spread_mask(mask_rows, channels):
    n, cols = mask_rows.shape
    eye = (
        lax.broadcasted_iota(jnp.int32, (cols, cols), 0)
        == lax.broadcasted_iota(jnp.int32, (cols, cols), 1)
    ).astype(F32)
    picked = (mask_rows[:, None, :] * eye[None]).astype(BF16).reshape(n * cols, cols)
    return jnp.dot(picked, jnp.ones((cols, channels), BF16), preferred_element_type=F32)


def branch_rows(triples, table, up, down):
    zonal = []
    n_taps = table.shape[0] - 1
    taps = [table[k : k + 1] for k in range(n_taps)]
    gain = table[n_taps:]
    for left, own, right in triples:
        cols = own.shape[0]
        start = cols - n_taps // 2 * DILATION_STEP
        line = jnp.concatenate([left, own, right], axis=0).astype(F32)
        aligned = shifted = None
        for k in range(n_taps):
            at = start + k * DILATION_STEP
            if at % 8 == 0:
                term = line[at : at + cols] * taps[k]
                aligned = term if aligned is None else aligned + term
            else:
                term = line[at - 4 : at - 4 + cols + 8] * taps[k]
                shifted = term if shifted is None else shifted + term
        zonal.append(aligned + shifted[4 : 4 + cols])
    zonal = jnp.concatenate(zonal, axis=0)
    mean = jnp.mean(zonal, axis=-1, keepdims=True)
    centred = zonal - mean
    var = jnp.mean(centred * centred, axis=-1, keepdims=True)
    normed = (centred * lax.rsqrt(var + 1e-6) * gain).astype(BF16)
    pre = jnp.dot(normed, up, preferred_element_type=F32)
    inner = pre * (0.7978845608028654 + (0.7978845608028654 * 0.044715) * (pre * pre))
    twice = (pre + pre * jnp.tanh(inner)).astype(BF16)
    return jnp.dot(twice, down, preferred_element_type=F32) * 0.5


def lead(tiles):
    return tiles * 7 // 16


def prep_kernel(
    slots, rows_hbm, owner_hbm, field_hbm, mask_hbm, masked, out_hbm,
    rows, owners, count, field, mask_t, mask_f, extra, extra_half, small_sems, load_sem, row_sems, extra_sem,
):
    lat_rows, cols, channels = field.shape
    tiles = out_hbm.shape[0]
    entries = owners.shape[0]
    small = [
        pltpu.make_async_copy(rows_hbm, rows, small_sems.at[0]),
        pltpu.make_async_copy(owner_hbm, owners, small_sems.at[1]),
        pltpu.make_async_copy(mask_hbm, mask_t, small_sems.at[2]),
    ]
    load = pltpu.make_async_copy(field_hbm, field, load_sem)
    for copy in small:
        copy.start()
    load.start()
    mask_f[...] = jnp.zeros_like(mask_f)
    extra[...] = jnp.zeros_like(extra)
    for tile in range(tiles):
        count[tile] = 0

    def row_copy(e, row, owner, rank):
        return pltpu.make_async_copy(
            masked.at[row],
            out_hbm.at[owner, pl.ds(pl.multiple_of(rank * cols, cols), cols)],
            row_sems.at[e],
        )

    for copy in small:
        copy.wait()
    mask = mask_t[...].astype(F32).T
    mask_f[:, :cols] = mask
    places = []
    for e in range(entries):
        owner = lax.rem(owners[e] + tiles - lead(tiles), tiles)
        row = rows[e]
        rank = count[owner]
        count[owner] = rank + 1
        extra[pl.ds(owner * EXTRA + rank, 1), :] = mask_f[pl.ds(row, 1), :]
        places.append((row, owner, rank))
    extra_half[...] = extra[...].astype(BF16).reshape(tiles, EXTRA, channels)
    extra_copy = pltpu.make_async_copy(extra_half, out_hbm.at[:, pl.ds(slots * cols, EXTRA)], extra_sem)
    extra_copy.start()
    wide = spread_mask(mask, channels).astype(BF16).reshape(lat_rows, cols, channels)
    load.wait()
    masked[...] = field[...] * wide
    for e, place in enumerate(places):
        row_copy(e, *place).start()
    for e, place in enumerate(places):
        row_copy(e, *place).wait()
    extra_copy.wait()


def prep(field, land_mask, polar_rows, polar_owner, tiles, slots):
    lat_rows, cols, channels = field.shape
    hbm = pl.BlockSpec(memory_space=pltpu.HBM)
    vmem = pl.BlockSpec(memory_space=pltpu.VMEM)
    return pl.pallas_call(
        functools.partial(prep_kernel, slots),
        out_shape=(
            pltpu.VMEM(field.shape, BF16),
            jax.ShapeDtypeStruct((tiles, slots * cols + EXTRA, channels), BF16),
        ),
        in_specs=[hbm] * 4,
        out_specs=(vmem, hbm),
        scratch_shapes=[
            pltpu.SMEM(polar_rows.shape, jnp.int32),
            pltpu.SMEM(polar_owner.shape, jnp.int32),
            pltpu.SMEM((tiles,), jnp.int32),
            pltpu.VMEM(field.shape, BF16),
            pltpu.VMEM((cols, lat_rows), jnp.int32),
            pltpu.VMEM((lat_rows, channels), F32),
            pltpu.VMEM((tiles * EXTRA, channels), F32),
            pltpu.VMEM((tiles, EXTRA, channels), BF16),
            pltpu.SemaphoreType.DMA((3,)),
            pltpu.SemaphoreType.DMA,
            pltpu.SemaphoreType.DMA(polar_owner.shape),
            pltpu.SemaphoreType.DMA,
        ],
        compiler_params=pltpu.CompilerParams(vmem_limit_bytes=PREP_VMEM_BYTES),
        cost_estimate=pl.CostEstimate(flops=10**6, bytes_accessed=2 * 10**6, transcendentals=0),
        name="prep",
    )(polar_rows, polar_owner, field, land_mask.T)


def side_kernel(polar_taps_ref, mask_ref, upper_ref, lower_ref, taps_ref, gain_ref, mask_f, near, table, bands_ref):
    half = upper_ref.shape[0]
    mask_f[...] = mask_ref[...].astype(F32).T
    near[:half] = upper_ref[...]
    near[half:] = lower_ref[...]
    table[: taps_ref.shape[0]] = taps_ref[...]
    table[taps_ref.shape[0] :] = gain_ref[...]
    n, depth = bands_ref.shape[0] // 2, bands_ref.shape[1]
    n_taps = polar_taps_ref.shape[0]
    offset = lax.broadcasted_iota(jnp.int32, (n, depth), 1) - lax.broadcasted_iota(jnp.int32, (n, depth), 0)
    first = (depth - n) // 2 - n_taps // 2
    band = jnp.zeros((n, depth), F32)
    for k in range(n_taps):
        band = jnp.where(offset == k + first, polar_taps_ref[k], band)
    high = band.astype(BF16)
    bands_ref[:n] = high
    bands_ref[n:] = (band - high.astype(F32)).astype(BF16)


def side_part(polar_taps, land_mask, swaps, zonal_tap_weight, norm_gain):
    lat_rows, cols = land_mask.shape
    smem = pl.BlockSpec(memory_space=pltpu.SMEM)
    vmem = pl.BlockSpec(memory_space=pltpu.VMEM)
    half, _, channels = swaps[0].shape
    return pl.pallas_call(
        side_kernel,
        out_shape=(
            jax.ShapeDtypeStruct((lat_rows, cols), F32),
            jax.ShapeDtypeStruct((2 * half, cols, channels), BF16),
            jax.ShapeDtypeStruct((zonal_tap_weight.shape[0] + 1, channels), F32),
            jax.ShapeDtypeStruct((256, 160), BF16),
        ),
        in_specs=[smem] + [vmem] * 5,
        out_specs=(vmem,) * 4,
        compiler_params=pltpu.CompilerParams(vmem_limit_bytes=VMEM_BYTES),
        cost_estimate=pl.CostEstimate(flops=10**6, bytes_accessed=10**6, transcendentals=0),
        name="side",
    )(polar_taps, land_mask.T, *swaps, zonal_tap_weight, norm_gain.reshape(1, channels))


def tile_kernel(own_ref, cross_ref, near_ref, mask_ref, table_ref, up_ref, down_ref, mixed_ref):
    lat_rows, cols, channels = own_ref.shape
    odd = lax.rem(lax.axis_index("lon"), 2)

    def all_rows(left, right):
        triples = [(left[r], own_ref[r], right[r]) for r in range(lat_rows)]
        branch = branch_rows(triples, table_ref[...], up_ref[...], down_ref[...])
        wide = spread_mask(mask_ref[...], channels)
        own = own_ref[...].reshape(lat_rows * cols, channels).astype(F32)
        mixed = wide * (own + branch.astype(BF16).astype(F32))
        mixed_ref[...] = mixed.astype(BF16).reshape(lat_rows, cols, channels)

    pl.when(odd == 0)(functools.partial(all_rows, cross_ref, near_ref))
    pl.when(odd == 1)(functools.partial(all_rows, near_ref, cross_ref))


def tile_part(masked, cross, near, mask_f, weights):
    vmem = pl.BlockSpec(memory_space=pltpu.VMEM)
    return pl.pallas_call(
        tile_kernel,
        out_shape=jax.ShapeDtypeStruct(masked.shape, BF16),
        in_specs=[vmem] * 7,
        out_specs=vmem,
        compiler_params=pltpu.CompilerParams(vmem_limit_bytes=VMEM_BYTES),
        cost_estimate=pl.CostEstimate(flops=TILE_FLOPS, bytes_accessed=3 * 10**6, transcendentals=10**6),
        name="tile",
    )(masked, cross, near, mask_f, *weights)


def polar_kernel(
    slots, cols, recv_ref, bands_ref, table_ref, up_ref, down_ref,
    out_hbm, circle, out, sems,
):
    tiles, _, channels = recv_ref.shape
    n, depth = bands_ref.shape[0] // 2, bands_ref.shape[1]
    pad = (depth - n) // 2
    nlon = tiles * cols
    first = lead(tiles)
    extra = recv_ref[:, slots * cols :, :].astype(F32)
    extra = jnp.concatenate([extra[tiles - first :], extra[: tiles - first]], axis=0)
    share = nlon // n // SHARES

    def out_copy(pair, part):
        at = (pl.ds(pair * 2, 2), pl.ds(part * share * n, share * n))
        return pltpu.make_async_copy(out.at[at], out_hbm.at[at], sems.at[pair, part])

    def filter_pair(pair):
        for half in range(2):
            slot = pair * 2 + half
            pieces = [
                recv_ref[(t - first) % tiles, slot * cols : (slot + 1) * cols, :].astype(F32) for t in range(tiles)
            ]
            triples = [(pieces[t - 1], pieces[t], pieces[(t + 1) % tiles]) for t in range(tiles)]
            branch = branch_rows(triples, table_ref[...], up_ref[...], down_ref[...])
            wide = spread_mask(extra[:, slot, :cols], channels)
            own = jnp.concatenate(pieces, axis=0)
            mixed = jnp.where(wide > 0.5, own + branch.astype(BF16).astype(F32), 0.0).astype(BF16)
            lanes = slice(half * channels, (half + 1) * channels)
            circle[pair, pad : nlon + pad, lanes] = mixed
            circle[pair, :pad, lanes] = mixed[nlon - pad :]
            circle[pair, nlon + pad :, lanes] = mixed[:pad]
        for b in range(nlon // n):
            both = jnp.dot(bands_ref[...], circle[pair, b * n : b * n + depth, :], preferred_element_type=F32)
            rows = (both[:n] + both[n:]).astype(BF16)
            for half in range(2):
                out[pair * 2 + half, b * n : (b + 1) * n, :] = rows[:, half * channels : (half + 1) * channels]
            if (b + 1) % share == 0:
                out_copy(pair, b // share).start()

    def clear_pair(pair):
        out[pair * 2 : pair * 2 + 2] = jnp.zeros_like(out[pair * 2 : pair * 2 + 2])
        for part in range(SHARES):
            out_copy(pair, part).start()

    pairs = slots // 2

    def all_pairs():
        for pair in range(pairs):
            filter_pair(pair)

    def first_pair():
        for pair in range(1, pairs):
            clear_pair(pair)
        filter_pair(0)

    if pairs > 1:
        ocean = jnp.max(extra[:, 2:slots, :])
        pl.when(ocean > 0.5)(all_pairs)
        pl.when(jnp.logical_not(ocean > 0.5))(first_pair)
    else:
        all_pairs()
    for pair in range(pairs):
        for part in range(SHARES):
            out_copy(pair, part).wait()


def polar_part(recv, bands, weights, slots, cols):
    tiles, _, channels = recv.shape
    vmem = pl.BlockSpec(memory_space=pltpu.VMEM)
    shape = (slots, tiles * cols, channels)
    return pl.pallas_call(
        functools.partial(polar_kernel, slots, cols),
        out_shape=jax.ShapeDtypeStruct(shape, BF16),
        in_specs=[vmem] * 5,
        out_specs=pl.BlockSpec(memory_space=pltpu.HBM),
        scratch_shapes=[
            pltpu.VMEM((slots // 2, tiles * cols + 32, 2 * channels), BF16),
            pltpu.VMEM(shape, BF16),
            pltpu.SemaphoreType.DMA((slots // 2, SHARES)),
        ],
        compiler_params=pltpu.CompilerParams(vmem_limit_bytes=VMEM_BYTES),
        cost_estimate=pl.CostEstimate(flops=6 * 10**8, bytes_accessed=2 * 10**6, transcendentals=10**6),
        name="polar",
    )(recv, bands, *weights)


def body(
    field,
    land_mask,
    zonal_tap_weight,
    norm_gain,
    up_weight,
    down_weight,
    polar_rows,
    polar_owner,
    polar_taps,
):
    lat_rows, cols, channels = field.shape
    tiles = lax.axis_size("lon")
    slots = max(2, lat_rows // tiles)
    masked, outgoing = prep(field, land_mask, polar_rows, polar_owner, tiles, slots)
    swap_pairs = [(i, i ^ 1) for i in range(tiles)]
    cross_pairs = [(i, (i + 1) % tiles if i % 2 else (i - 1) % tiles) for i in range(tiles)]
    cross = lax.ppermute(masked, "lon", cross_pairs)
    half = lat_rows // 2
    swaps = [lax.ppermute(masked[:half], "lon", swap_pairs), lax.ppermute(masked[half:], "lon", swap_pairs)]
    order = [(lead(tiles) + i) % tiles for i in range(tiles)]
    recv = lax.all_to_all(
        outgoing, "lon", split_axis=0, concat_axis=0, axis_index_groups=[order], tiled=True
    )
    mask_f, near, table, bands = side_part(polar_taps, land_mask, swaps, zonal_tap_weight, norm_gain)
    weights = (table, up_weight, down_weight)
    mixed = tile_part(masked, cross, near, mask_f, weights)
    polar = polar_part(recv, bands, weights, slots, cols)
    return (mixed, polar)


def solution(mesh):
    in_specs = (P("lat", "lon", None), P("lat", "lon"), P(), P(), P(), P(), P("lat"), P("lat"), P())
    out_specs = (P("lat", "lon", None), P(("lat", "lon"), None, None))
    return jax.shard_map(body, mesh=mesh, in_specs=in_specs, out_specs=out_specs, check_vma=False)
```

```python
import functools

import jax
import jax.numpy as jnp
from jax import lax
from jax.experimental import pallas as pl
from jax.experimental.pallas import tpu as pltpu
from jax.sharding import PartitionSpec as P

DILATION_STEP = 4
EXTRA = 8
TILE_FLOPS = 11 * 10**9
PARTS = 1
SHARES = 2
VMEM_BYTES = 48 * 1024 * 1024
PREP_VMEM_BYTES = 62 * 1024 * 1024
F32 = jnp.float32
BF16 = jnp.bfloat16


def spread_mask(mask_rows, channels):
    n, cols = mask_rows.shape
    eye = (
        lax.broadcasted_iota(jnp.int32, (cols, cols), 0)
        == lax.broadcasted_iota(jnp.int32, (cols, cols), 1)
    ).astype(F32)
    picked = (mask_rows[:, None, :] * eye[None]).astype(BF16).reshape(n * cols, cols)
    return jnp.dot(picked, jnp.ones((cols, channels), BF16), preferred_element_type=F32)


def branch_rows(triples, table, up, down):
    zonal = []
    n_taps = table.shape[0] - 1
    taps = [table[k : k + 1] for k in range(n_taps)]
    gain = table[n_taps:]
    for left, own, right in triples:
        cols = own.shape[0]
        start = cols - n_taps // 2 * DILATION_STEP
        line = jnp.concatenate([left, own, right], axis=0).astype(F32)
        aligned = shifted = None
        for k in range(n_taps):
            at = start + k * DILATION_STEP
            if at % 8 == 0:
                term = line[at : at + cols] * taps[k]
                aligned = term if aligned is None else aligned + term
            else:
                term = line[at - 4 : at - 4 + cols + 8] * taps[k]
                shifted = term if shifted is None else shifted + term
        zonal.append(aligned + shifted[4 : 4 + cols])
    zonal = jnp.concatenate(zonal, axis=0)
    mean = jnp.mean(zonal, axis=-1, keepdims=True)
    centred = zonal - mean
    var = jnp.mean(centred * centred, axis=-1, keepdims=True)
    normed = (centred * lax.rsqrt(var + 1e-6) * gain).astype(BF16)
    pre = jnp.dot(normed, up, preferred_element_type=F32)
    inner = pre * (0.7978845608028654 + (0.7978845608028654 * 0.044715) * (pre * pre))
    twice = (pre + pre * jnp.tanh(inner)).astype(BF16)
    return jnp.dot(twice, down, preferred_element_type=F32) * 0.5


def lead(tiles):
    return tiles * 7 // 16


def prep_kernel(
    slots, halo, rows_hbm, owner_hbm, field_hbm, mask_hbm, masked, edge, out_hbm,
    rows, owners, count, field, mask_t, mask_f, extra, extra_half, small_sems, load_sem, row_sems, extra_sem,
):
    lat_rows, cols, channels = field.shape
    tiles = out_hbm.shape[0]
    entries = owners.shape[0]
    small = [
        pltpu.make_async_copy(rows_hbm, rows, small_sems.at[0]),
        pltpu.make_async_copy(owner_hbm, owners, small_sems.at[1]),
        pltpu.make_async_copy(mask_hbm, mask_t, small_sems.at[2]),
    ]
    load = pltpu.make_async_copy(field_hbm, field, load_sem)
    for copy in small:
        copy.start()
    load.start()
    mask_f[...] = jnp.zeros_like(mask_f)
    extra[...] = jnp.zeros_like(extra)
    for tile in range(tiles):
        count[tile] = 0

    def row_copy(e, row, owner, rank):
        return pltpu.make_async_copy(
            masked.at[row],
            out_hbm.at[owner, pl.ds(pl.multiple_of(rank * cols, cols), cols)],
            row_sems.at[e],
        )

    for copy in small:
        copy.wait()
    mask = mask_t[...].astype(F32).T
    mask_f[:, :cols] = mask
    places = []
    for e in range(entries):
        owner = lax.rem(owners[e] + tiles - lead(tiles), tiles)
        row = rows[e]
        rank = count[owner]
        count[owner] = rank + 1
        extra[pl.ds(owner * EXTRA + rank, 1), :] = mask_f[pl.ds(row, 1), :]
        places.append((row, owner, rank))
    extra_half[...] = extra[...].astype(BF16).reshape(tiles, EXTRA, channels)
    extra_copy = pltpu.make_async_copy(extra_half, out_hbm.at[:, pl.ds(slots * cols, EXTRA)], extra_sem)
    extra_copy.start()
    wide = spread_mask(mask, channels).astype(BF16).reshape(lat_rows, cols, channels)
    load.wait()
    masked[...] = field[...] * wide
    for e, place in enumerate(places):
        row_copy(e, *place).start()
    odd = lax.rem(lax.axis_index("lon"), 2)

    def pack(start):
        for g in range(lat_rows // 4):
            parts = [masked[g * 4 + q].astype(F32)[start : start + halo] for q in range(4)]
            edge[g] = jnp.concatenate(parts, axis=0).astype(BF16)

    pl.when(odd == 0)(functools.partial(pack, 0))
    pl.when(odd == 1)(functools.partial(pack, cols - halo))
    for e, place in enumerate(places):
        row_copy(e, *place).wait()
    extra_copy.wait()


def prep(field, land_mask, polar_rows, polar_owner, tiles, slots, halo):
    lat_rows, cols, channels = field.shape
    hbm = pl.BlockSpec(memory_space=pltpu.HBM)
    vmem = pl.BlockSpec(memory_space=pltpu.VMEM)
    return pl.pallas_call(
        functools.partial(prep_kernel, slots, halo),
        out_shape=(
            pltpu.VMEM(field.shape, BF16),
            pltpu.VMEM((lat_rows // 4, 4 * halo, channels), BF16),
            jax.ShapeDtypeStruct((tiles, slots * cols + EXTRA, channels), BF16),
        ),
        in_specs=[hbm] * 4,
        out_specs=(vmem, vmem, hbm),
        scratch_shapes=[
            pltpu.SMEM(polar_rows.shape, jnp.int32),
            pltpu.SMEM(polar_owner.shape, jnp.int32),
            pltpu.SMEM((tiles,), jnp.int32),
            pltpu.VMEM(field.shape, BF16),
            pltpu.VMEM((cols, lat_rows), jnp.int32),
            pltpu.VMEM((lat_rows, channels), F32),
            pltpu.VMEM((tiles * EXTRA, channels), F32),
            pltpu.VMEM((tiles, EXTRA, channels), BF16),
            pltpu.SemaphoreType.DMA((3,)),
            pltpu.SemaphoreType.DMA,
            pltpu.SemaphoreType.DMA(polar_owner.shape),
            pltpu.SemaphoreType.DMA,
        ],
        compiler_params=pltpu.CompilerParams(vmem_limit_bytes=PREP_VMEM_BYTES),
        cost_estimate=pl.CostEstimate(flops=10**6, bytes_accessed=2 * 10**6, transcendentals=0),
        name="prep",
    )(polar_rows, polar_owner, field, land_mask.T)


def side_kernel(polar_taps_ref, mask_ref, upper_ref, lower_ref, taps_ref, gain_ref, mask_f, near, table, bands_ref):
    half = upper_ref.shape[0]
    mask_f[...] = mask_ref[...].astype(F32).T
    near[:half] = upper_ref[...]
    near[half:] = lower_ref[...]
    table[: taps_ref.shape[0]] = taps_ref[...]
    table[taps_ref.shape[0] :] = gain_ref[...]
    n, depth = bands_ref.shape[0] // 2, bands_ref.shape[1]
    n_taps = polar_taps_ref.shape[0]
    offset = lax.broadcasted_iota(jnp.int32, (n, depth), 1) - lax.broadcasted_iota(jnp.int32, (n, depth), 0)
    first = (depth - n) // 2 - n_taps // 2
    band = jnp.zeros((n, depth), F32)
    for k in range(n_taps):
        band = jnp.where(offset == k + first, polar_taps_ref[k], band)
    high = band.astype(BF16)
    bands_ref[:n] = high
    bands_ref[n:] = (band - high.astype(F32)).astype(BF16)


def side_part(polar_taps, land_mask, swaps, zonal_tap_weight, norm_gain):
    lat_rows, cols = land_mask.shape
    smem = pl.BlockSpec(memory_space=pltpu.SMEM)
    vmem = pl.BlockSpec(memory_space=pltpu.VMEM)
    half, _, channels = swaps[0].shape
    return pl.pallas_call(
        side_kernel,
        out_shape=(
            jax.ShapeDtypeStruct((lat_rows, cols), F32),
            jax.ShapeDtypeStruct((2 * half, cols, channels), BF16),
            jax.ShapeDtypeStruct((zonal_tap_weight.shape[0] + 1, channels), F32),
            jax.ShapeDtypeStruct((256, 160), BF16),
        ),
        in_specs=[smem] + [vmem] * 5,
        out_specs=(vmem,) * 4,
        compiler_params=pltpu.CompilerParams(vmem_limit_bytes=VMEM_BYTES),
        cost_estimate=pl.CostEstimate(flops=10**6, bytes_accessed=10**6, transcendentals=0),
        name="side",
    )(polar_taps, land_mask.T, *swaps, zonal_tap_weight, norm_gain.reshape(1, channels))


def tile_kernel(own_ref, cross_ref, near_ref, mask_ref, table_ref, up_ref, down_ref, mixed_ref):
    lat_rows, cols, channels = own_ref.shape
    odd = lax.rem(lax.axis_index("lon"), 2)

    def all_rows(left, right):
        triples = [(left(r), own_ref[r].astype(F32), right(r)) for r in range(lat_rows)]
        branch = branch_rows(triples, table_ref[...], up_ref[...], down_ref[...])
        wide = spread_mask(mask_ref[...], channels)
        own = own_ref[...].reshape(lat_rows * cols, channels).astype(F32)
        mixed = wide * (own + branch.astype(BF16).astype(F32))
        mixed_ref[...] = mixed.astype(BF16).reshape(lat_rows, cols, channels)

    halo = cross_ref.shape[1] // 4
    rest = jnp.zeros((cols - halo, channels), F32)

    def near(r):
        return near_ref[r].astype(F32)

    def far(r):
        return cross_ref[r // 4].astype(F32)[r % 4 * halo : (r % 4 + 1) * halo]

    def far_left(r):
        return jnp.concatenate([rest, far(r)], axis=0)

    def far_right(r):
        return jnp.concatenate([far(r), rest], axis=0)

    pl.when(odd == 0)(functools.partial(all_rows, far_left, near))
    pl.when(odd == 1)(functools.partial(all_rows, near, far_right))


def tile_part(masked, cross, near, mask_f, weights):
    vmem = pl.BlockSpec(memory_space=pltpu.VMEM)
    return pl.pallas_call(
        tile_kernel,
        out_shape=jax.ShapeDtypeStruct(masked.shape, BF16),
        in_specs=[vmem] * 7,
        out_specs=vmem,
        compiler_params=pltpu.CompilerParams(vmem_limit_bytes=VMEM_BYTES),
        cost_estimate=pl.CostEstimate(flops=TILE_FLOPS, bytes_accessed=3 * 10**6, transcendentals=10**6),
        name="tile",
    )(masked, cross, near, mask_f, *weights)


def polar_kernel(
    slots, cols, recv_ref, bands_ref, table_ref, up_ref, down_ref,
    out_hbm, circle, out, sems,
):
    tiles, _, channels = recv_ref.shape
    n, depth = bands_ref.shape[0] // 2, bands_ref.shape[1]
    pad = (depth - n) // 2
    nlon = tiles * cols
    first = lead(tiles)
    extra = recv_ref[:, slots * cols :, :].astype(F32)
    extra = jnp.concatenate([extra[tiles - first :], extra[: tiles - first]], axis=0)
    share = nlon // n // SHARES

    def out_copy(pair, part):
        at = (pl.ds(pair * 2, 2), pl.ds(part * share * n, share * n))
        return pltpu.make_async_copy(out.at[at], out_hbm.at[at], sems.at[pair, part])

    def filter_pair(pair):
        for half in range(2):
            slot = pair * 2 + half
            pieces = [
                recv_ref[(t - first) % tiles, slot * cols : (slot + 1) * cols, :].astype(F32) for t in range(tiles)
            ]
            triples = [(pieces[t - 1], pieces[t], pieces[(t + 1) % tiles]) for t in range(tiles)]
            branch = branch_rows(triples, table_ref[...], up_ref[...], down_ref[...])
            wide = spread_mask(extra[:, slot, :cols], channels)
            own = jnp.concatenate(pieces, axis=0)
            mixed = jnp.where(wide > 0.5, own + branch.astype(BF16).astype(F32), 0.0).astype(BF16)
            lanes = slice(half * channels, (half + 1) * channels)
            circle[pair, pad : nlon + pad, lanes] = mixed
            circle[pair, :pad, lanes] = mixed[nlon - pad :]
            circle[pair, nlon + pad :, lanes] = mixed[:pad]
        for b in range(nlon // n):
            both = jnp.dot(bands_ref[...], circle[pair, b * n : b * n + depth, :], preferred_element_type=F32)
            rows = (both[:n] + both[n:]).astype(BF16)
            for half in range(2):
                out[pair * 2 + half, b * n : (b + 1) * n, :] = rows[:, half * channels : (half + 1) * channels]
            if (b + 1) % share == 0:
                out_copy(pair, b // share).start()

    def clear_pair(pair):
        out[pair * 2 : pair * 2 + 2] = jnp.zeros_like(out[pair * 2 : pair * 2 + 2])
        for part in range(SHARES):
            out_copy(pair, part).start()

    pairs = slots // 2

    def all_pairs():
        for pair in range(pairs):
            filter_pair(pair)

    def first_pair():
        for pair in range(1, pairs):
            clear_pair(pair)
        filter_pair(0)

    if pairs > 1:
        ocean = jnp.max(extra[:, 2:slots, :])
        pl.when(ocean > 0.5)(all_pairs)
        pl.when(jnp.logical_not(ocean > 0.5))(first_pair)
    else:
        all_pairs()
    for pair in range(pairs):
        for part in range(SHARES):
            out_copy(pair, part).wait()


def polar_part(recv, bands, weights, slots, cols):
    tiles, _, channels = recv.shape
    vmem = pl.BlockSpec(memory_space=pltpu.VMEM)
    shape = (slots, tiles * cols, channels)
    return pl.pallas_call(
        functools.partial(polar_kernel, slots, cols),
        out_shape=jax.ShapeDtypeStruct(shape, BF16),
        in_specs=[vmem] * 5,
        out_specs=pl.BlockSpec(memory_space=pltpu.HBM),
        scratch_shapes=[
            pltpu.VMEM((slots // 2, tiles * cols + 32, 2 * channels), BF16),
            pltpu.VMEM(shape, BF16),
            pltpu.SemaphoreType.DMA((slots // 2, SHARES)),
        ],
        compiler_params=pltpu.CompilerParams(vmem_limit_bytes=VMEM_BYTES),
        cost_estimate=pl.CostEstimate(flops=6 * 10**8, bytes_accessed=2 * 10**6, transcendentals=10**6),
        name="polar",
    )(recv, bands, *weights)


def body(
    field,
    land_mask,
    zonal_tap_weight,
    norm_gain,
    up_weight,
    down_weight,
    polar_rows,
    polar_owner,
    polar_taps,
):
    lat_rows, cols, channels = field.shape
    tiles = lax.axis_size("lon")
    slots = max(2, lat_rows // tiles)
    halo = zonal_tap_weight.shape[0] // 2 * DILATION_STEP
    masked, edge, outgoing = prep(field, land_mask, polar_rows, polar_owner, tiles, slots, halo)
    swap_pairs = [(i, i ^ 1) for i in range(tiles)]
    cross_pairs = [(i, (i + 1) % tiles if i % 2 else (i - 1) % tiles) for i in range(tiles)]
    cross = lax.ppermute(edge, "lon", cross_pairs)
    half = lat_rows // 2
    swaps = [lax.ppermute(masked[:half], "lon", swap_pairs), lax.ppermute(masked[half:], "lon", swap_pairs)]
    order = [(lead(tiles) + i) % tiles for i in range(tiles)]
    recv = lax.all_to_all(
        outgoing, "lon", split_axis=0, concat_axis=0, axis_index_groups=[order], tiled=True
    )
    mask_f, near, table, bands = side_part(polar_taps, land_mask, swaps, zonal_tap_weight, norm_gain)
    weights = (table, up_weight, down_weight)
    mixed = tile_part(masked, cross, near, mask_f, weights)
    polar = polar_part(recv, bands, weights, slots, cols)
    return (mixed, polar)


def solution(mesh):
    in_specs = (P("lat", "lon", None), P("lat", "lon"), P(), P(), P(), P(), P("lat"), P("lat"), P())
    out_specs = (P("lat", "lon", None), P(("lat", "lon"), None, None))
    return jax.shard_map(body, mesh=mesh, in_specs=in_specs, out_specs=out_specs, check_vma=False)
```

```python
import functools

import jax
import jax.numpy as jnp
from jax import lax
from jax.experimental import pallas as pl
from jax.experimental.pallas import tpu as pltpu
from jax.sharding import PartitionSpec as P

DILATION_STEP = 4
EXTRA = 8
TILE_FLOPS = 9 * 10**9
PARTS = 1
SHARES = 2
VMEM_BYTES = 48 * 1024 * 1024
PREP_VMEM_BYTES = 62 * 1024 * 1024
F32 = jnp.float32
BF16 = jnp.bfloat16


def spread_mask(mask_rows, channels):
    n, cols = mask_rows.shape
    eye = (
        lax.broadcasted_iota(jnp.int32, (cols, cols), 0)
        == lax.broadcasted_iota(jnp.int32, (cols, cols), 1)
    ).astype(F32)
    picked = (mask_rows[:, None, :] * eye[None]).astype(BF16).reshape(n * cols, cols)
    return jnp.dot(picked, jnp.ones((cols, channels), BF16), preferred_element_type=F32)


def branch_rows(triples, table, up, down):
    zonal = []
    n_taps = table.shape[0] - 1
    taps = [table[k : k + 1] for k in range(n_taps)]
    gain = table[n_taps:]
    for left, own, right in triples:
        cols = own.shape[0]
        start = cols - n_taps // 2 * DILATION_STEP
        line = jnp.concatenate([left, own, right], axis=0).astype(F32)
        aligned = shifted = None
        for k in range(n_taps):
            at = start + k * DILATION_STEP
            if at % 8 == 0:
                term = line[at : at + cols] * taps[k]
                aligned = term if aligned is None else aligned + term
            else:
                term = line[at - 4 : at - 4 + cols + 8] * taps[k]
                shifted = term if shifted is None else shifted + term
        zonal.append(aligned + shifted[4 : 4 + cols])
    zonal = jnp.concatenate(zonal, axis=0)
    mean = jnp.mean(zonal, axis=-1, keepdims=True)
    centred = zonal - mean
    var = jnp.mean(centred * centred, axis=-1, keepdims=True)
    normed = (centred * lax.rsqrt(var + 1e-6) * gain).astype(BF16)
    pre = jnp.dot(normed, up, preferred_element_type=F32)
    inner = pre * (0.7978845608028654 + (0.7978845608028654 * 0.044715) * (pre * pre))
    twice = (pre + pre * jnp.tanh(inner)).astype(BF16)
    return jnp.dot(twice, down, preferred_element_type=F32) * 0.5


def lead(tiles):
    return tiles * 9 // 16


def prep_kernel(
    slots, halo, rows_hbm, owner_hbm, field_hbm, mask_hbm, masked, edge, out_hbm,
    rows, owners, count, field, mask_t, mask_f, extra, extra_half, small_sems, load_sem, row_sems, extra_sem,
):
    lat_rows, cols, channels = field.shape
    tiles = out_hbm.shape[0]
    entries = owners.shape[0]
    small = [
        pltpu.make_async_copy(rows_hbm, rows, small_sems.at[0]),
        pltpu.make_async_copy(owner_hbm, owners, small_sems.at[1]),
        pltpu.make_async_copy(mask_hbm, mask_t, small_sems.at[2]),
    ]
    load = pltpu.make_async_copy(field_hbm, field, load_sem)
    for copy in small:
        copy.start()
    load.start()
    mask_f[...] = jnp.zeros_like(mask_f)
    extra[...] = jnp.zeros_like(extra)
    for tile in range(tiles):
        count[tile] = 0

    def row_copy(e, row, owner, rank):
        return pltpu.make_async_copy(
            masked.at[row],
            out_hbm.at[owner, pl.ds(pl.multiple_of(rank * cols, cols), cols)],
            row_sems.at[e],
        )

    for copy in small:
        copy.wait()
    mask = mask_t[...].astype(F32).T
    mask_f[:, :cols] = mask
    places = []
    for e in range(entries):
        owner = lax.rem(owners[e] + tiles - lead(tiles), tiles)
        row = rows[e]
        rank = count[owner]
        count[owner] = rank + 1
        extra[pl.ds(owner * EXTRA + rank, 1), :] = mask_f[pl.ds(row, 1), :]
        places.append((row, owner, rank))
    extra_half[...] = extra[...].astype(BF16).reshape(tiles, EXTRA, channels)
    extra_copy = pltpu.make_async_copy(extra_half, out_hbm.at[:, pl.ds(slots * cols, EXTRA)], extra_sem)
    extra_copy.start()
    wide = spread_mask(mask, channels).astype(BF16).reshape(lat_rows, cols, channels)
    load.wait()
    masked[...] = field[...] * wide
    for e, place in enumerate(places):
        row_copy(e, *place).start()
    odd = lax.rem(lax.axis_index("lon"), 2)

    def pack(start):
        for g in range(lat_rows // 4):
            parts = [masked[g * 4 + q].astype(F32)[start : start + halo] for q in range(4)]
            edge[g] = jnp.concatenate(parts, axis=0).astype(BF16)

    pl.when(odd == 0)(functools.partial(pack, 0))
    pl.when(odd == 1)(functools.partial(pack, cols - halo))
    for e, place in enumerate(places):
        row_copy(e, *place).wait()
    extra_copy.wait()


def prep(field, land_mask, polar_rows, polar_owner, tiles, slots, halo):
    lat_rows, cols, channels = field.shape
    hbm = pl.BlockSpec(memory_space=pltpu.HBM)
    vmem = pl.BlockSpec(memory_space=pltpu.VMEM)
    return pl.pallas_call(
        functools.partial(prep_kernel, slots, halo),
        out_shape=(
            pltpu.VMEM(field.shape, BF16),
            pltpu.VMEM((lat_rows // 4, 4 * halo, channels), BF16),
            jax.ShapeDtypeStruct((tiles, slots * cols + EXTRA, channels), BF16),
        ),
        in_specs=[hbm] * 4,
        out_specs=(vmem, vmem, hbm),
        scratch_shapes=[
            pltpu.SMEM(polar_rows.shape, jnp.int32),
            pltpu.SMEM(polar_owner.shape, jnp.int32),
            pltpu.SMEM((tiles,), jnp.int32),
            pltpu.VMEM(field.shape, BF16),
            pltpu.VMEM((cols, lat_rows), jnp.int32),
            pltpu.VMEM((lat_rows, channels), F32),
            pltpu.VMEM((tiles * EXTRA, channels), F32),
            pltpu.VMEM((tiles, EXTRA, channels), BF16),
            pltpu.SemaphoreType.DMA((3,)),
            pltpu.SemaphoreType.DMA,
            pltpu.SemaphoreType.DMA(polar_owner.shape),
            pltpu.SemaphoreType.DMA,
        ],
        compiler_params=pltpu.CompilerParams(vmem_limit_bytes=PREP_VMEM_BYTES),
        cost_estimate=pl.CostEstimate(flops=10**6, bytes_accessed=2 * 10**6, transcendentals=0),
        name="prep",
    )(polar_rows, polar_owner, field, land_mask.T)


def side_kernel(polar_taps_ref, mask_ref, first_ref, second_ref, third_ref, fourth_ref, taps_ref, gain_ref, mask_f, near, table, bands_ref):
    part = first_ref.shape[0]
    mask_f[...] = mask_ref[...].astype(F32).T
    for p, ref in enumerate((first_ref, second_ref, third_ref, fourth_ref)):
        near[p * part : (p + 1) * part] = ref[...]
    table[: taps_ref.shape[0]] = taps_ref[...]
    table[taps_ref.shape[0] :] = gain_ref[...]
    n, depth = bands_ref.shape[0] // 2, bands_ref.shape[1]
    n_taps = polar_taps_ref.shape[0]
    offset = lax.broadcasted_iota(jnp.int32, (n, depth), 1) - lax.broadcasted_iota(jnp.int32, (n, depth), 0)
    first = (depth - n) // 2 - n_taps // 2
    band = jnp.zeros((n, depth), F32)
    for k in range(n_taps):
        band = jnp.where(offset == k + first, polar_taps_ref[k], band)
    high = band.astype(BF16)
    bands_ref[:n] = high
    bands_ref[n:] = (band - high.astype(F32)).astype(BF16)


def side_part(polar_taps, land_mask, swaps, zonal_tap_weight, norm_gain):
    lat_rows, cols = land_mask.shape
    smem = pl.BlockSpec(memory_space=pltpu.SMEM)
    vmem = pl.BlockSpec(memory_space=pltpu.VMEM)
    part, _, channels = swaps[0].shape
    return pl.pallas_call(
        side_kernel,
        out_shape=(
            jax.ShapeDtypeStruct((lat_rows, cols), F32),
            jax.ShapeDtypeStruct((4 * part, cols, channels), BF16),
            jax.ShapeDtypeStruct((zonal_tap_weight.shape[0] + 1, channels), F32),
            jax.ShapeDtypeStruct((256, 160), BF16),
        ),
        in_specs=[smem] + [vmem] * 7,
        out_specs=(vmem,) * 4,
        compiler_params=pltpu.CompilerParams(vmem_limit_bytes=VMEM_BYTES),
        cost_estimate=pl.CostEstimate(flops=10**6, bytes_accessed=10**6, transcendentals=0),
        name="side",
    )(polar_taps, land_mask.T, *swaps, zonal_tap_weight, norm_gain.reshape(1, channels))


def tile_kernel(own_ref, cross_ref, near_ref, mask_ref, table_ref, up_ref, down_ref, mixed_ref):
    lat_rows, cols, channels = own_ref.shape
    odd = lax.rem(lax.axis_index("lon"), 2)

    def all_rows(left, right):
        triples = [(left(r), own_ref[r].astype(F32), right(r)) for r in range(lat_rows)]
        branch = branch_rows(triples, table_ref[...], up_ref[...], down_ref[...])
        wide = spread_mask(mask_ref[...], channels)
        own = own_ref[...].reshape(lat_rows * cols, channels).astype(F32)
        mixed = wide * (own + branch.astype(BF16).astype(F32))
        mixed_ref[...] = mixed.astype(BF16).reshape(lat_rows, cols, channels)

    halo = cross_ref.shape[1] // 4
    rest = jnp.zeros((cols - halo, channels), F32)

    def near(r):
        return near_ref[r].astype(F32)

    def far(r):
        return cross_ref[r // 4].astype(F32)[r % 4 * halo : (r % 4 + 1) * halo]

    def far_left(r):
        return jnp.concatenate([rest, far(r)], axis=0)

    def far_right(r):
        return jnp.concatenate([far(r), rest], axis=0)

    pl.when(odd == 0)(functools.partial(all_rows, far_left, near))
    pl.when(odd == 1)(functools.partial(all_rows, near, far_right))


def tile_part(masked, cross, near, mask_f, weights):
    vmem = pl.BlockSpec(memory_space=pltpu.VMEM)
    return pl.pallas_call(
        tile_kernel,
        out_shape=jax.ShapeDtypeStruct(masked.shape, BF16),
        in_specs=[vmem] * 7,
        out_specs=vmem,
        compiler_params=pltpu.CompilerParams(vmem_limit_bytes=VMEM_BYTES),
        cost_estimate=pl.CostEstimate(flops=TILE_FLOPS, bytes_accessed=3 * 10**6, transcendentals=10**6),
        name="tile",
    )(masked, cross, near, mask_f, *weights)


def polar_kernel(
    slots, cols, recv_ref, bands_ref, table_ref, up_ref, down_ref,
    out_hbm, circle, out, sems,
):
    tiles, _, channels = recv_ref.shape
    n, depth = bands_ref.shape[0] // 2, bands_ref.shape[1]
    pad = (depth - n) // 2
    nlon = tiles * cols
    first = lead(tiles)
    extra = recv_ref[:, slots * cols :, :].astype(F32)
    extra = jnp.concatenate([extra[tiles - first :], extra[: tiles - first]], axis=0)
    share = nlon // n // SHARES

    def out_copy(pair, part):
        at = (pl.ds(pair * 2, 2), pl.ds(part * share * n, share * n))
        return pltpu.make_async_copy(out.at[at], out_hbm.at[at], sems.at[pair, part])

    def filter_pair(pair):
        for half in range(2):
            slot = pair * 2 + half
            pieces = [
                recv_ref[(t - first) % tiles, slot * cols : (slot + 1) * cols, :].astype(F32) for t in range(tiles)
            ]
            triples = [(pieces[t - 1], pieces[t], pieces[(t + 1) % tiles]) for t in range(tiles)]
            branch = branch_rows(triples, table_ref[...], up_ref[...], down_ref[...])
            wide = spread_mask(extra[:, slot, :cols], channels)
            own = jnp.concatenate(pieces, axis=0)
            mixed = jnp.where(wide > 0.5, own + branch.astype(BF16).astype(F32), 0.0).astype(BF16)
            lanes = slice(half * channels, (half + 1) * channels)
            circle[pair, pad : nlon + pad, lanes] = mixed
            circle[pair, :pad, lanes] = mixed[nlon - pad :]
            circle[pair, nlon + pad :, lanes] = mixed[:pad]
        for b in range(nlon // n):
            both = jnp.dot(bands_ref[...], circle[pair, b * n : b * n + depth, :], preferred_element_type=F32)
            rows = (both[:n] + both[n:]).astype(BF16)
            for half in range(2):
                out[pair * 2 + half, b * n : (b + 1) * n, :] = rows[:, half * channels : (half + 1) * channels]
            if (b + 1) % share == 0:
                out_copy(pair, b // share).start()

    def clear_pair(pair):
        out[pair * 2 : pair * 2 + 2] = jnp.zeros_like(out[pair * 2 : pair * 2 + 2])
        for part in range(SHARES):
            out_copy(pair, part).start()

    pairs = slots // 2

    def all_pairs():
        for pair in range(pairs):
            filter_pair(pair)

    def first_pair():
        for pair in range(1, pairs):
            clear_pair(pair)
        filter_pair(0)

    if pairs > 1:
        ocean = jnp.max(extra[:, 2:slots, :])
        pl.when(ocean > 0.5)(all_pairs)
        pl.when(jnp.logical_not(ocean > 0.5))(first_pair)
    else:
        all_pairs()
    for pair in range(pairs):
        for part in range(SHARES):
            out_copy(pair, part).wait()


def polar_part(recv, bands, weights, slots, cols):
    tiles, _, channels = recv.shape
    vmem = pl.BlockSpec(memory_space=pltpu.VMEM)
    shape = (slots, tiles * cols, channels)
    return pl.pallas_call(
        functools.partial(polar_kernel, slots, cols),
        out_shape=jax.ShapeDtypeStruct(shape, BF16),
        in_specs=[vmem] * 5,
        out_specs=pl.BlockSpec(memory_space=pltpu.HBM),
        scratch_shapes=[
            pltpu.VMEM((slots // 2, tiles * cols + 32, 2 * channels), BF16),
            pltpu.VMEM(shape, BF16),
            pltpu.SemaphoreType.DMA((slots // 2, SHARES)),
        ],
        compiler_params=pltpu.CompilerParams(vmem_limit_bytes=VMEM_BYTES),
        cost_estimate=pl.CostEstimate(flops=6 * 10**8, bytes_accessed=2 * 10**6, transcendentals=10**6),
        name="polar",
    )(recv, bands, *weights)


def body(
    field,
    land_mask,
    zonal_tap_weight,
    norm_gain,
    up_weight,
    down_weight,
    polar_rows,
    polar_owner,
    polar_taps,
):
    lat_rows, cols, channels = field.shape
    tiles = lax.axis_size("lon")
    slots = max(2, lat_rows // tiles)
    halo = zonal_tap_weight.shape[0] // 2 * DILATION_STEP
    masked, edge, outgoing = prep(field, land_mask, polar_rows, polar_owner, tiles, slots, halo)
    swap_pairs = [(i, i ^ 1) for i in range(tiles)]
    cross_pairs = [(i, (i + 1) % tiles if i % 2 else (i - 1) % tiles) for i in range(tiles)]
    cross = lax.ppermute(edge, "lon", cross_pairs)
    part = lat_rows // 4
    swaps = [lax.ppermute(masked[p * part : (p + 1) * part], "lon", swap_pairs) for p in range(4)]
    order = [(lead(tiles) + i) % tiles for i in range(tiles)]
    recv = lax.all_to_all(
        outgoing, "lon", split_axis=0, concat_axis=0, axis_index_groups=[order], tiled=True
    )
    mask_f, near, table, bands = side_part(polar_taps, land_mask, swaps, zonal_tap_weight, norm_gain)
    weights = (table, up_weight, down_weight)
    mixed = tile_part(masked, cross, near, mask_f, weights)
    polar = polar_part(recv, bands, weights, slots, cols)
    return (mixed, polar)


def solution(mesh):
    in_specs = (P("lat", "lon", None), P("lat", "lon"), P(), P(), P(), P(), P("lat"), P("lat"), P())
    out_specs = (P("lat", "lon", None), P(("lat", "lon"), None, None))
    return jax.shard_map(body, mesh=mesh, in_specs=in_specs, out_specs=out_specs, check_vma=False)
```
